256 devices in a mesh: dp: 4 (over z_hi, core), space: 64 (over y, x, z_lo).
Axes of the slice: x: 4, y: 4, z: 8 (z_hi: 2, z_lo: 4; z = z_hi * 4 + z_lo), core: 2. Of those that a mesh axis runs over, the one named last changes fastest.
Arguments:
- activations: bfloat16 [4, 32, 256, 16, 128], P('dp', None, 'space'), may hold values from -16 to 16
- cotangent: bfloat16 [4, 32, 256, 16, 128], P('dp', None, 'space'), may hold values from -16 to 16
- weight: bfloat16 [32, 864], replicated, may hold values from -0.21875 to 0.21875
Outputs:
- conv_out: bfloat16 [4, 32, 256, 16, 128], P('dp', None, 'space')
- input_grad: bfloat16 [4, 32, 256, 16, 128], P('dp', None, 'space')
- precond_grad: float32 [32, 864], replicated
The draws below stay inside these ranges and needn't reach their ends.
All inputs are finite; a program needn't handle non-finite values. Where the reference program divides by a largest or mean magnitude, that divisor is 1e-20 or more.
Results may differ from the reference program's by a relative error of at most 0.0049.
Values may be sent and summed in bfloat16 or wider, within the bound.
No kernel may reach another device: no remote copies, remote signals or barrier semaphores. Data moves between devices by JAX's collectives and lax.ppermute only.
A program may use at most 64 MiB of HBM per device.

```python
import math
import jax
import jax.numpy as jnp
from jax import lax

C = 32
K = 864
SLAB = 4
NY = 16
NZ = 128
ITERS = 3
BATCH = 4
NX = 256
CELLS = 2097152


def channel_bumps(key, plane_count, slab_planes, channel_count):
    centers = jax.random.uniform(key, (1, channel_count, 1, 1, 1), jnp.float32, 0.0, 1.0) * plane_count
    positions = jnp.arange(plane_count, dtype=jnp.float32).reshape(1, 1, plane_count, 1, 1) + 0.5
    width = 1.5 * slab_planes
    distance = (positions - centers) / width
    return 1.0 + 5.0 * jnp.exp(-0.5 * distance * distance)


def draw_activations(key, part):
    key = jax.random.fold_in(key, 11)
    subkeys = jax.random.split(key, 5)
    full_shape = (BATCH, C, NX, NY, NZ)
    noise_base = jax.random.normal(subkeys[0], full_shape, jnp.float32)
    spread = math.log(4.0)
    mixture = noise_base + 0.6 * jnp.roll(noise_base, 1, axis=2) + 0.5 * jnp.roll(noise_base, 1, axis=3) + 0.4 * jnp.roll(noise_base, 1, axis=1)
    scales = jnp.exp(jax.random.uniform(subkeys[1], (1, C, 1, 1, 1), jnp.float32, 0.0, spread))
    x_ramp = 1.0 + 2.0 * jnp.arange(NX, dtype=jnp.float32).reshape(1, 1, NX, 1, 1) / max(NX - 1, 1)
    roughness = jax.random.uniform(subkeys[2], full_shape, jnp.float32, 0.6, 1.4)
    bumps = channel_bumps(subkeys[4], NX, SLAB, C)
    values = mixture * scales * x_ramp * roughness * bumps / 3.0
    return jnp.clip(values, -16.0, 16.0).astype(jnp.bfloat16)


def draw_cotangent(key, part):
    key = jax.random.fold_in(key, 23)
    subkeys = jax.random.split(key, 5)
    full_shape = (BATCH, C, NX, NY, NZ)
    noise_base = jax.random.normal(subkeys[0], full_shape, jnp.float32)
    spread = math.log(4.0)
    mixture = noise_base + 0.3 * jnp.roll(noise_base, 1, axis=1) + 0.4 * jnp.roll(noise_base, 1, axis=4)
    scales = jnp.exp(jax.random.uniform(subkeys[1], (1, C, 1, 1, 1), jnp.float32, 0.0, spread))
    x_ramp = 1.0 + 2.0 * jnp.arange(NX, dtype=jnp.float32).reshape(1, 1, NX, 1, 1) / max(NX - 1, 1)
    roughness = jax.random.uniform(subkeys[2], full_shape, jnp.float32, 0.6, 1.4)
    bumps = channel_bumps(subkeys[4], NX, SLAB, C)
    values = mixture * scales * x_ramp * roughness * bumps / 2.0
    return jnp.clip(values, -16.0, 16.0).astype(jnp.bfloat16)


def scatter_about(own_key, extent, deviation, bound, kind=jnp.bfloat16):
    values = jax.random.normal(own_key, extent, jnp.float32) * deviation
    return jnp.minimum(jnp.maximum(values, -bound), bound).astype(kind)


def setup_inputs(seed: int = 0) -> dict:
    key_of = jax.random.split(jax.random.key(seed), 4)
    activations = draw_activations(jax.random.fold_in(key_of[3], 71), 0)
    cotangent = draw_cotangent(jax.random.fold_in(key_of[3], 71), 0)
    weight = scatter_about(key_of[2], (C, K), K ** -0.5, 0.21875)
    return {"activations": activations, "cotangent": cotangent, "weight": weight}


DAMPING = 0.1
block_rows = 8

def shift_depth(volume, offset):
    widths = [(0, 0)] * (volume.ndim - 1)
    if offset < 0:
        return jnp.pad(volume[..., :-1], widths + [(1, 0)])
    if offset > 0:
        return jnp.pad(volume[..., 1:], widths + [(0, 1)])
    return volume

def block_patches(source, plane_at, row_at):
    zero_index = jnp.asarray(0, jnp.int32)
    window = lax.dynamic_slice(source, (zero_index, plane_at, row_at, zero_index), (source.shape[0], 3, block_rows + 2, source.shape[3]))
    pieces = []
    for first in range(3):
        for second in range(3):
            for third_tap in range(3):
                pieces.append(shift_depth(window[:, first, second:second + block_rows, :], third_tap - 1))
    stacked = jnp.stack(pieces, 0)
    return stacked.reshape(27 * source.shape[0], block_rows * source.shape[3])

def newton_inverse(factor, order_size):
    eye_matrix = jnp.eye(order_size, dtype=jnp.float32)
    scaled = factor * (order_size / jnp.trace(factor)) + DAMPING * eye_matrix
    row_bound = jnp.max(lax.optimization_barrier(jnp.sum(jnp.abs(scaled), axis=1)))
    iterate = eye_matrix / row_bound
    for sweep in range(ITERS):
        left_part = jnp.dot(iterate, scaled, precision=lax.Precision.HIGHEST)
        iterate = 2.0 * iterate - jnp.dot(left_part, iterate, precision=lax.Precision.HIGHEST)
    return iterate

def reference(activations, cotangent, weight):
    both = jnp.stack([activations, cotangent], 0)
    padded = jnp.pad(both, ((0, 0), (0, 0), (0, 0), (1, 1), (1, 1), (0, 0)))
    flipped = weight.reshape(C, 27, C)[:, ::-1, :].transpose(2, 1, 0).reshape(C, 27 * C)
    blocks = NY // block_rows
    contract = (((1,), (1,)), ((), ()))

    def step(carry, counter):
        act_sum, grad_sum, wgrad_sum = carry
        sample = counter // (NX * blocks)
        remain = counter % (NX * blocks)
        plane_at = (remain // blocks).astype(jnp.int32)
        row_at = (remain % blocks * block_rows).astype(jnp.int32)
        volumes = lax.dynamic_index_in_dim(padded, sample, 1, keepdims=False)
        act_patch = block_patches(volumes[0], plane_at, row_at)
        cot_patch = block_patches(volumes[1], plane_at, row_at)
        center = cot_patch[13 * C:14 * C]
        out_block = jnp.dot(weight, act_patch, preferred_element_type=jnp.float32).astype(jnp.bfloat16)
        back_block = jnp.dot(flipped, cot_patch, preferred_element_type=jnp.float32).astype(jnp.bfloat16)
        act_sum = act_sum + lax.dot_general(act_patch, act_patch, contract, preferred_element_type=jnp.float32)
        grad_sum = grad_sum + lax.dot_general(center, center, contract, preferred_element_type=jnp.float32)
        wgrad_sum = wgrad_sum + lax.dot_general(center, act_patch, contract, preferred_element_type=jnp.float32)
        return ((act_sum, grad_sum, wgrad_sum), (out_block, back_block))
    start_carry = (jnp.zeros((K, K), jnp.float32), jnp.zeros((C, C), jnp.float32), jnp.zeros((C, K), jnp.float32))
    sums, results = lax.scan(step, start_carry, jnp.arange(BATCH * NX * blocks, dtype=jnp.int32))
    act_sum, grad_sum, wgrad_sum = sums

    def arrange(stacked_blocks):
        shaped = stacked_blocks.reshape(BATCH, NX, blocks, C, block_rows, NZ)
        return shaped.transpose(0, 3, 1, 2, 4, 5).reshape(BATCH, C, NX, NY, NZ)
    conv_out = arrange(results[0])
    input_grad = arrange(results[1])
    act_factor = act_sum / CELLS
    grad_factor = grad_sum / CELLS
    weight_grad = wgrad_sum / CELLS
    inverse_act = newton_inverse(act_factor, K)
    inverse_grad = newton_inverse(grad_factor, C)
    right_part = jnp.dot(weight_grad, inverse_act, precision=lax.Precision.HIGHEST)
    applied = jnp.dot(inverse_grad, right_part, precision=lax.Precision.HIGHEST)
    quadratic = jnp.sum(applied * weight_grad)
    precond_grad = applied * jnp.sqrt(C * K / quadratic)
    return (conv_out, input_grad, precond_grad)
```

```python
import functools

import jax
import jax.numpy as jnp
from jax import lax
from jax.experimental import pallas as pl
from jax.experimental.pallas import tpu as pltpu
from jax.sharding import Mesh
from jax.sharding import PartitionSpec as P

ITERS = 3
DAMPING = 0.1
C = 32
PLANES = 4
ROWS = 16
LANES = 128
RPAD = ROWS + 4
TAPS = 3 * C
ORDER = 27 * C
WIDE = 9 * LANES
CELLS = 2097152
MIB = 1024 * 1024
NT = (((1,), (1,)), ((), ()))
f32 = jnp.float32
bf16 = jnp.bfloat16


CLASSES = []
for _x in ("0", "f", "l"):
    for _y in ("0", "f", "l", 1, 2):
        CLASSES.append((_x, _y))
for _x in (1, 2):
    for _y in ("0", "f", "l", 1, 2, -1, -2):
        CLASSES.append((_x, _y))
SLOT = {key: index for index, key in enumerate(CLASSES)}
GRAD = 27
BLOCKS = 32
HALF = BLOCKS // 2


def lane(row):
    return row * LANES


def fill_taps(dst, col, plane, rows=ROWS):
    flat = plane.reshape(rows * C, LANES)
    wide = flat.astype(f32)
    at = lax.broadcasted_iota(jnp.int32, wide.shape, 1)
    before = jnp.where(at == 0, 0.0, pltpu.roll(wide, 1, 1)).astype(bf16)
    after = jnp.where(at == LANES - 1, 0.0, pltpu.roll(wide, LANES - 1, 1)).astype(bf16)
    for y in range(rows):
        here = pl.ds(col + lane(y), LANES)
        part = slice(y * C, (y + 1) * C)
        dst[0:C, here] = before[part]
        dst[C : 2 * C, here] = flat[part]
        dst[2 * C : 3 * C, here] = after[part]


def fill_rows(dst, col, plane):
    for y in range(ROWS):
        dst[:, pl.ds(col + lane(y), LANES)] = plane[y]


def zero_rows(dst, col):
    zero = jnp.zeros((dst.shape[0], 2 * LANES), dst.dtype)
    dst[:, pl.ds(col, 2 * LANES)] = zero
    dst[:, pl.ds(col + lane(ROWS + 2), 2 * LANES)] = zero


def plane_at(index, row=0):
    return lane(index * RPAD + 2 + row)


def dot_nt(left, right):
    return lax.dot_general(left, right, NT, preferred_element_type=f32)


WIDTH = ROWS * LANES


def shifted(ref, index, rows, width=WIDTH):
    return jnp.concatenate([ref[:, pl.ds(plane_at(index, dy), width)] for dy in rows], 0)


A_P0, A_P3, A_X0 = 0, 5, 10
A_X1, A_X2 = 15, 22
A_BLOCKS = 29


def gram_inner(act_ref, cot_ref, out_ref, wg_ref, taps, cots):
    for x in range(PLANES):
        col = lane(x * RPAD)
        zero_rows(taps, col)
        zero_rows(cots, col)
        fill_taps(taps, plane_at(x), act_ref[x])
        fill_rows(cots, plane_at(x), cot_ref[x])

    def put(slot, value):
        out_ref[slot] = value

    def blocks(value, count):
        return [value[i * TAPS : (i + 1) * TAPS] for i in range(count)]

    near = (-1, 0, 1)
    sums = {}

    def add(key, value):
        sums[key] = value if key not in sums else sums[key] + value

    for x in range(PLANES):
        stay = jnp.concatenate(
            [taps[:, pl.ds(plane_at(x), WIDTH)], cots[:, pl.ds(plane_at(x), WIDTH)]], 0
        )
        level = dot_nt(shifted(taps, x, (0, 1, 2)), stay)
        zero, one, two = blocks(level, 3)
        cot_rows = [dot_nt(shifted(cots, x, near), stay)]
        if x + 1 < PLANES:
            up = dot_nt(shifted(taps, x + 1, (0, 1, 2, -1, -2)), stay)
            add("x1", up)
            cot_rows.append(dot_nt(shifted(cots, x + 1, near), stay))
            add("w2", cot_rows[1])
        if x >= 1:
            add("w0", dot_nt(shifted(cots, x - 1, near), stay))
        add("w1", cot_rows[0])
        if x + 2 < PLANES:
            add("x2", dot_nt(shifted(taps, x + 2, (0, 1, 2, -1, -2)), stay))
        edge = {}
        for name, row in (("F", 0), ("L", ROWS - 1)):
            stay_row = taps[:, pl.ds(plane_at(x, row), LANES)]
            count = min(3, PLANES - x)
            moving = jnp.concatenate(
                [taps[:, pl.ds(plane_at(x + i, row), LANES)] for i in range(count)], 0
            )
            edge_sum = blocks(jnp.pad(dot_nt(moving, stay_row), ((0, 0), (0, C))), count)
            edge[name] = edge_sum[0]
            for i in range(1, count):
                add((name, i), edge_sum[i])
        for i, value in enumerate((zero, edge["F"], edge["L"], one, two)):
            add(("level", i), value)
            if x == 0:
                put(A_P0 + i, value)
            if x == PLANES - 1:
                put(A_P3 + i, value)
    for i in range(5):
        put(A_X0 + i, sums[("level", i)])
    for base, name, i in ((A_X1, "x1", 1), (A_X2, "x2", 2)):
        whole = blocks(sums[name], 5)
        for j, value in enumerate((whole[0], sums[("F", i)], sums[("L", i)], *whole[1:])):
            put(base + j, value)
    wg_ref[0] = sums["w2"]
    wg_ref[1] = sums["w1"]
    wg_ref[2] = sums["w0"]


def gram_outer(
    core_ref, first_ref, last_ref, in_ref, wg_ref, act_ref, low_ref, high_ref, cot_ref,
    keep_ref, send_ref, taps, cots, out_ref,
):
    for index in range(6):
        zero_rows(taps, lane(index * RPAD))
        if index in (0, 2, 3, 4, 5):
            plane = low_ref[0] if index == 0 else high_ref[0] if index == 5 else act_ref[index - 1]
            fill_taps(taps, plane_at(index), plane)
    for slot, x in ((0, 0), (1, 3)):
        zero_rows(cots, lane(slot * RPAD))
        fill_rows(cots, plane_at(slot), cot_ref[x])

    def stay(index):
        return taps[:, pl.ds(plane_at(index), WIDTH)]

    five = (0, 1, 2, -1, -2)
    near = (-1, 0, 1)
    own = core_ref[0]
    first = first_ref[0].astype(f32)
    last = last_ref[0].astype(f32)

    def blocks(value, count):
        return [value[i * TAPS : (i + 1) * TAPS] for i in range(count)]

    def padded(value):
        return jnp.concatenate([value, jnp.zeros((value.shape[0], LANES - TAPS), f32)], 1)

    low = stay(0)
    gap = jnp.zeros((LANES - TAPS, WIDTH), bf16)
    top = dot_nt(shifted(taps, 5, five), jnp.concatenate([stay(4), gap, stay(3), gap], 0))
    x1 = blocks(top[:, :LANES], 5)
    x2 = blocks(top[:, LANES:] + dot_nt(shifted(taps, 2, five), jnp.concatenate([low, gap], 0)), 5)
    w_low = dot_nt(shifted(cots, 0, near), low)
    w_high = dot_nt(shifted(cots, 1, near), stay(5))

    def edge(left, right, row):
        return padded(dot_nt(
            taps[:, pl.ds(plane_at(left, row), LANES)], taps[:, pl.ds(plane_at(right, row), LANES)]
        ))

    wide = jnp.zeros((TAPS, LANES - TAPS), f32)
    wsums = (
        wg_ref[0] + jnp.concatenate([w_low, wide], 1),
        wg_ref[1],
        wg_ref[2] + jnp.concatenate([w_high, wide], 1),
    )
    at = lax.broadcasted_iota(jnp.int32, (TAPS, LANES), 1)

    def piece(t):
        if t > GRAD:
            return jnp.zeros((C, LANES), f32)
        if t == GRAD:
            return wsums[1][C : 2 * C]
        a, b, c = t // 9, t // 3 % 3, t % 3
        return pltpu.roll(wsums[a][(2 - b) * C : (3 - b) * C], TAPS - c * C, 1)

    def put(slot, value):
        extra = piece(slot)
        high = extra.astype(bf16).astype(f32)
        extra = jnp.concatenate([high, extra - high, jnp.zeros((C, LANES), f32)], 0)
        out_ref[(slot // HALF) ^ own, slot % HALF] = jnp.where(at < TAPS, value, extra).astype(bf16)

    def cut(value):
        return value

    for base, dx, parts, pairs in (
        (A_X1, 1, x1, ((5, 4),)),
        (A_X2, 2, x2, ((5, 3), (2, 0))),
    ):
        whole = cut(in_ref[base]) + parts[0]
        put(SLOT[(dx, "0")], whole)
        for j, (name, row) in enumerate((("f", 0), ("l", ROWS - 1))):
            edge_sum = cut(in_ref[base + 1 + j])
            for left, right in pairs:
                edge_sum = edge_sum + edge(left, right, row)
            put(SLOT[(dx, name)], whole - edge_sum)
        for j, dy in enumerate((1, 2, -1, -2)):
            put(SLOT[(dx, dy)], cut(in_ref[base + 3 + j]) + parts[1 + j])
    for name in ("0", "f", "l"):
        values = [cut(in_ref[A_X0 + i]) for i in range(5)]
        if name == "f":
            values = [v - first * cut(in_ref[A_P0 + i]) for i, v in enumerate(values)]
        if name == "l":
            values = [v - last * cut(in_ref[A_P3 + i]) for i, v in enumerate(values)]
        put(SLOT[(name, "0")], values[0])
        put(SLOT[(name, "f")], values[0] - values[1])
        put(SLOT[(name, "l")], values[0] - values[2])
        put(SLOT[(name, 1)], values[3])
        put(SLOT[(name, 2)], values[4])
    for slot in range(len(CLASSES), BLOCKS):
        put(slot, jnp.zeros((TAPS, LANES), f32))
    keep_ref[...] = out_ref[0]
    send_ref[...] = out_ref[1]


def settle(value):
    at = lax.broadcasted_iota(jnp.int32, (C, LANES), 1)
    first, second = value[:C], value[C : 2 * C]
    both = first + second
    high = both.astype(bf16).astype(f32)
    first = jnp.where(at < TAPS, first, high)
    second = jnp.where(at < TAPS, second, both - high)
    return jnp.concatenate([first, second, value[2 * C :]], 0).astype(bf16)


def add_kernel(keep_ref, arrived_ref, out_ref):
    for i in range(HALF):
        out_ref[i] = settle(keep_ref[i].astype(f32) + arrived_ref[i].astype(f32))


def sum_kernel(parts_ref, out_ref):
    total = parts_ref[0].astype(f32)
    for i in range(1, parts_ref.shape[0]):
        total = total + parts_ref[i].astype(f32)
    total = settle(total)
    for i in range(out_ref.shape[0]):
        out_ref[i] = total


def conv_kernel(which, x_ref, low_ref, high_ref, w_ref, out_ref, taps):
    for index in range(PLANES + 2):
        zero_rows(taps, lane(index * RPAD))
        plane = low_ref[which] if index == 0 else high_ref[which] if index == PLANES + 1 else x_ref[index - 1]
        fill_taps(taps, plane_at(index), plane)
    weight = w_ref[...]
    step = 2
    for x in range(PLANES):
        for y in range(0, ROWS, step):
            patch = jnp.concatenate(
                [
                    taps[:, pl.ds(plane_at(x + 1 + dx, y + dy), step * LANES)]
                    for dx in (-1, 0, 1)
                    for dy in (-1, 0, 1)
                ],
                0,
            )
            value = jnp.dot(weight, patch, preferred_element_type=f32).astype(bf16)
            for i in range(step):
                out_ref[x, y + i] = value[:, lane(i) : lane(i + 1)]


def split(value):
    high = value.astype(bf16)
    return high, (value - high.astype(f32)).astype(bf16)


def class_of(offset):
    return {0: "0", 1: "f", -1: "l"}[offset]


def finish_kernel(core_ref, mine_ref, other_ref, out_ref, both, factor):
    own = core_ref[0]
    both[own] = mine_ref[...]
    both[1 - own] = other_ref[...]

    def block(slot):
        return both[slot // HALF, slot % HALF]

    at = lax.broadcasted_iota(jnp.int32, (TAPS, LANES), 1)
    offsets = [(a, b) for a in (-1, 0, 1) for b in (-1, 0, 1)]
    tail = jnp.zeros((LANES - TAPS, LANES), bf16)
    cache = {}

    def padded(slot):
        if slot not in cache:
            value = jnp.where(at < TAPS, block(slot), jnp.zeros((), bf16))
            full = jnp.concatenate([value, tail], 0)
            cache[slot] = (full, full.T)
        return cache[slot]

    for i, (ax, ay) in enumerate(offsets):
        for j, (bx, by) in enumerate(offsets):
            dx, dy = bx - ax, by - ay
            if dx < 0 or (dx == 0 and dy < 0):
                continue
            key = (class_of(ax) if dx == 0 else dx, class_of(ay) if dy == 0 else dy)
            full, turned = padded(SLOT[key])
            factor[lane(j) : lane(j + 1), lane(i) : lane(i + 1)] = full
            if i != j:
                factor[lane(i) : lane(i + 1), lane(j) : lane(j + 1)] = turned

    def extra(t):
        here = both.at[t // HALF, t % HALF]
        return here[0:C, :].astype(f32) + here[C : 2 * C, :].astype(f32)

    pieces = []
    for i in range(9):
        rows = jnp.zeros((C, LANES), f32)
        for c in range(3):
            moved = pltpu.roll(extra(3 * i + c), C + c * C, 1)
            rows = jnp.where(at[:C] // C == c, moved, rows)
        pieces.append(rows)
    wgrad = jnp.concatenate(pieces, 1) * (1.0 / CELLS)

    grad = extra(GRAD)[:, TAPS:LANES]
    row_id = lax.broadcasted_iota(jnp.int32, (C, C), 0)
    col_id = lax.broadcasted_iota(jnp.int32, (C, C), 1)
    eye = jnp.where(row_id == col_id, 1.0, 0.0).astype(f32)
    scaled = grad * (C / jnp.sum(grad * eye)) + DAMPING * eye
    bound = jnp.max(jnp.sum(jnp.abs(scaled), axis=1))
    inverse = eye / bound
    for _ in range(ITERS):
        half = jnp.dot(inverse, scaled, precision=lax.Precision.HIGHEST, preferred_element_type=f32)
        inverse = 2.0 * inverse - jnp.dot(
            half, inverse, precision=lax.Precision.HIGHEST, preferred_element_type=f32
        )

    trace = jnp.zeros((), f32)
    sums = jnp.zeros((1, WIDE), f32)
    diag_row = lax.broadcasted_iota(jnp.int32, (LANES, LANES), 0)
    diag_col = lax.broadcasted_iota(jnp.int32, (LANES, LANES), 1)
    diagonal = jnp.zeros((LANES, LANES), f32)
    for i in range(9):
        rows = factor[lane(i) : lane(i + 1), :].astype(f32)
        sums = sums + jnp.sum(jnp.abs(rows), axis=0, keepdims=True)
        diagonal = diagonal + jnp.where(diag_row == diag_col, rows[:, lane(i) : lane(i + 1)], 0.0)
    trace = jnp.sum(diagonal)
    scale = ORDER / trace
    bound = scale * jnp.max(sums) + DAMPING
    step = scale / bound
    keep = 1.0 - DAMPING / bound
    value = wgrad
    for _ in range(2**ITERS - 1):
        high, low = split(value)
        product = jnp.dot(jnp.concatenate([high, low], 0), factor[...], preferred_element_type=f32)
        value = wgrad + keep * value - step * (product[:C] + product[C:])
    right = value * (1.0 / bound)
    applied = jnp.dot(inverse, right, precision=lax.Precision.HIGHEST, preferred_element_type=f32)
    quadratic = jnp.sum(applied * wgrad)
    result = applied * jnp.sqrt(C * ORDER / quadratic)
    out_ref[...] = jnp.concatenate([result[:, lane(i) : lane(i) + TAPS] for i in range(9)], 1)


SMEM = pl.BlockSpec(memory_space=pltpu.SMEM)
WHOLE = pl.BlockSpec(memory_space=pltpu.VMEM)


def call(kernel, shapes, scratch, inputs, scalars=0, flops=0, mib=16):
    return pl.pallas_call(
        kernel,
        out_shape=shapes,
        in_specs=[SMEM] * scalars + [WHOLE] * (len(inputs) - scalars),
        out_specs=jax.tree.map(lambda _: WHOLE, shapes),
        scratch_shapes=scratch,
        compiler_params=pltpu.CompilerParams(vmem_limit_bytes=mib * MIB),
        cost_estimate=pl.CostEstimate(flops=flops, bytes_accessed=1 << 20, transcendentals=0),
    )(*inputs)


def conv(which, planes, low, high, weight):
    return call(
        functools.partial(conv_kernel, which),
        jax.ShapeDtypeStruct(planes.shape, bf16),
        [pltpu.VMEM((TAPS, 6 * RPAD * LANES), bf16)],
        (planes, low, high, weight),
        flops=2 * C * ORDER * PLANES * ROWS * LANES,
    )


def body(activations, cotangent, weight):
    space = ("y", "x", "z_lo")
    size = lax.axis_size(space)
    up = [(i, i + 1) for i in range(size - 1)]
    down = [(j, i) for i, j in up]

    def outer_planes(x):
        pair = jnp.stack([activations[0, :, x], cotangent[0, :, x]], 0)
        return pair.transpose(0, 2, 1, 3)

    low = lax.ppermute(outer_planes(PLANES - 1), space, up)
    high = lax.ppermute(outer_planes(0), space, down)
    act = activations[0].transpose(1, 2, 0, 3)
    cot = cotangent[0].transpose(1, 2, 0, 3)
    where = lax.axis_index(space)
    core = lax.axis_index("core").astype(jnp.int32).reshape(1)
    first = (where == 0).astype(jnp.int32).reshape(1)
    last = (where == size - 1).astype(jnp.int32).reshape(1)

    sums, wsums = call(
        gram_inner,
        (
            jax.ShapeDtypeStruct((A_BLOCKS, TAPS, LANES), f32),
            jax.ShapeDtypeStruct((3, TAPS, LANES), f32),
        ),
        [
            pltpu.VMEM((TAPS, PLANES * RPAD * LANES), bf16),
            pltpu.VMEM((C, PLANES * RPAD * LANES), bf16),
        ],
        (act, cot),
        flops=24 * 10**9 // 4,
        mib=24,
    )
    blocks_half = jax.ShapeDtypeStruct((HALF, TAPS, LANES), bf16)
    keep, send = call(
        gram_outer,
        (blocks_half, blocks_half),
        [
            pltpu.VMEM((TAPS, 6 * RPAD * LANES), bf16),
            pltpu.VMEM((C, 2 * RPAD * LANES), bf16),
            pltpu.VMEM((2, HALF, TAPS, LANES), bf16),
        ],
        (core, first, last, sums, wsums, act, low, high, cot),
        scalars=3,
        flops=10**9,
        mib=24,
    )

    hold = lax.optimization_barrier
    swap = [(0, 1), (1, 0)]
    arrived = lax.ppermute(send, "core", swap)
    mine = call(add_kernel, blocks_half, [], (keep, arrived), mib=4)
    mine, act, low, high, weight = hold((mine, act, low, high, weight))
    parts = lax.all_to_all(mine, ("y", "x"), 0, 0, tiled=True)
    out = conv(0, act, low, high, weight)
    flipped = weight.reshape(C, 27, C)[:, ::-1, :].transpose(2, 1, 0).reshape(C, ORDER)
    parts, out, flipped = hold((parts, out, flipped))
    depth = lax.axis_size(("z_hi", "z_lo"))
    block = call(sum_kernel, jax.ShapeDtypeStruct((depth, TAPS, LANES), bf16), [], (parts,), mib=4)
    block, cot, low, high = hold((block, cot, low, high))
    parts = lax.all_to_all(block, ("z_hi", "z_lo"), 0, 0, tiled=True)
    back = conv(1, cot, low, high, flipped)
    parts, back = hold((parts, back))
    block = call(sum_kernel, blocks_half, [], (parts,), mib=4)
    block, out, back = hold((block, out, back))
    whole = lax.all_to_all(block, ("y", "x"), 0, 0, tiled=True)

    def arrange(planes):
        return planes.transpose(2, 0, 1, 3)[None]

    out, back = arrange(out), arrange(back)
    whole, out, back = hold((whole, out, back))
    other = lax.ppermute(whole, "core", swap)
    precond = call(
        finish_kernel,
        jax.ShapeDtypeStruct((C, ORDER), f32),
        [pltpu.VMEM((2, HALF, TAPS, LANES), bf16), pltpu.VMEM((WIDE, WIDE), bf16)],
        (core, whole, other),
        scalars=1,
        flops=10**9,
    )
    return out, back, precond


def solution(mesh):
    fine = Mesh(mesh.devices.reshape(2, 2, 4, 4, 4), ("z_hi", "core", "y", "x", "z_lo"))
    spec = P(("z_hi", "core"), None, ("y", "x", "z_lo"), None, None)
    return jax.shard_map(
        body,
        mesh=fine,
        in_specs=(spec, spec, P()),
        out_specs=(spec, spec, P()),
        check_vma=False,
    )
```

```python
import functools

import jax
import jax.numpy as jnp
from jax import lax
from jax.experimental import pallas as pl
from jax.experimental.pallas import tpu as pltpu
from jax.sharding import Mesh
from jax.sharding import PartitionSpec as P

ITERS = 3
DAMPING = 0.1
C = 32
PLANES = 4
ROWS = 16
LANES = 128
RPAD = ROWS + 4
TAPS = 3 * C
ORDER = 27 * C
WIDE = 9 * LANES
CELLS = 2097152
MIB = 1024 * 1024
MIB_INNER, MIB_OUTER = 16, 16
NT = (((1,), (1,)), ((), ()))
f32 = jnp.float32
bf16 = jnp.bfloat16


CLASSES = []
for _x in ("0", "f", "l"):
    for _y in ("0", "f", "l", 1, 2):
        CLASSES.append((_x, _y))
for _x in (1, 2):
    for _y in ("0", "f", "l", 1, 2, -1, -2):
        CLASSES.append((_x, _y))
SLOT = {key: index for index, key in enumerate(CLASSES)}
GRAD = 27
BLOCKS = 32
HALF = BLOCKS // 2


def lane(row):
    return row * LANES


def turned(plane, store):
    store[...] = plane.astype(f32).reshape(C * ROWS, LANES)
    return [store[pl.ds(y, C, stride=ROWS), :] for y in range(ROWS)]


def rows_of(plane):
    return [plane[y].astype(f32) for y in range(ROWS)]


def fill_taps(dst, col, rows):
    at = lax.broadcasted_iota(jnp.int32, (C, LANES), 1)
    for y in range(ROWS):
        here = pl.ds(col + lane(y), LANES)
        before = jnp.where(at == 0, 0.0, pltpu.roll(rows[y], 1, 1))
        after = jnp.where(at == LANES - 1, 0.0, pltpu.roll(rows[y], LANES - 1, 1))
        dst[0:C, here] = before.astype(bf16)
        dst[C : 2 * C, here] = rows[y].astype(bf16)
        dst[2 * C : 3 * C, here] = after.astype(bf16)


def fill_rows(dst, col, rows):
    for y in range(ROWS):
        dst[:, pl.ds(col + lane(y), LANES)] = rows[y].astype(bf16)


def zero_rows(dst, col):
    zero = jnp.zeros((dst.shape[0], 2 * LANES), dst.dtype)
    dst[:, pl.ds(col, 2 * LANES)] = zero
    dst[:, pl.ds(col + lane(ROWS + 2), 2 * LANES)] = zero


def plane_at(index, row=0):
    return lane(index * RPAD + 2 + row)


def dot_nt(left, right):
    return lax.dot_general(left, right, NT, preferred_element_type=f32)


WIDTH = ROWS * LANES


def shifted(ref, index, rows, width=WIDTH):
    return jnp.concatenate([ref[:, pl.ds(plane_at(index, dy), width)] for dy in rows], 0)


A_P0, A_P3, A_X0 = 0, 5, 10
A_X1, A_X2 = 15, 22
A_BLOCKS = 29


def gram_inner(
    act_hbm, cot_hbm, out_ref, wg_ref, turned_act, turned_cot,
    taps, cots, store, act_ref, cot_ref, sems,
):
    fetches = []
    for x in range(PLANES):
        for i, (source, target) in enumerate(((act_hbm, act_ref), (cot_hbm, cot_ref))):
            fetches.append(
                pltpu.make_async_copy(source.at[:, x], target.at[x], sems.at[2 * x + i])
            )
    for fetch in fetches:
        fetch.start()
    for x in range(PLANES):
        zero_rows(taps, lane(x * RPAD))
        zero_rows(cots, lane(x * RPAD))
    for x in range(PLANES):
        fetches[2 * x].wait()
        fetches[2 * x + 1].wait()
        rows = turned(act_ref[x], store.at[2 * x])
        fill_taps(taps, plane_at(x), rows)
        cot_rows = turned(cot_ref[x], store.at[2 * x + 1])
        fill_rows(cots, plane_at(x), cot_rows)
        for y in range(ROWS):
            turned_act[x, y] = rows[y].astype(bf16)
            turned_cot[x, y] = cot_rows[y].astype(bf16)

    def put(slot, value):
        out_ref[slot] = value

    def blocks(value, count):
        return [value[i * TAPS : (i + 1) * TAPS] for i in range(count)]

    near = (-1, 0, 1)
    sums = {}

    def add(key, value):
        sums[key] = value if key not in sums else sums[key] + value

    for x in range(PLANES):
        stay = jnp.concatenate(
            [taps[:, pl.ds(plane_at(x), WIDTH)], cots[:, pl.ds(plane_at(x), WIDTH)]], 0
        )
        level = dot_nt(shifted(taps, x, (0, 1, 2)), stay)
        zero, one, two = blocks(level, 3)
        cot_rows = [dot_nt(shifted(cots, x, near), stay)]
        if x + 1 < PLANES:
            up = dot_nt(shifted(taps, x + 1, (0, 1, 2, -1, -2)), stay)
            add("x1", up)
            cot_rows.append(dot_nt(shifted(cots, x + 1, near), stay))
            add("w2", cot_rows[1])
        if x >= 1:
            add("w0", dot_nt(shifted(cots, x - 1, near), stay))
        add("w1", cot_rows[0])
        if x + 2 < PLANES:
            add("x2", dot_nt(shifted(taps, x + 2, (0, 1, 2, -1, -2)), stay))
        edge = {}
        for name, row in (("F", 0), ("L", ROWS - 1)):
            stay_row = taps[:, pl.ds(plane_at(x, row), LANES)]
            count = min(3, PLANES - x)
            moving = jnp.concatenate(
                [taps[:, pl.ds(plane_at(x + i, row), LANES)] for i in range(count)], 0
            )
            edge_sum = blocks(jnp.pad(dot_nt(moving, stay_row), ((0, 0), (0, C))), count)
            edge[name] = edge_sum[0]
            for i in range(1, count):
                add((name, i), edge_sum[i])
        for i, value in enumerate((zero, edge["F"], edge["L"], one, two)):
            add(("level", i), value)
            if x == 0:
                put(A_P0 + i, value)
            if x == PLANES - 1:
                put(A_P3 + i, value)
    for i in range(5):
        put(A_X0 + i, sums[("level", i)])
    for base, name, i in ((A_X1, "x1", 1), (A_X2, "x2", 2)):
        whole = blocks(sums[name], 5)
        for j, value in enumerate((whole[0], sums[("F", i)], sums[("L", i)], *whole[1:])):
            put(base + j, value)
    wg_ref[0] = sums["w2"]
    wg_ref[1] = sums["w1"]
    wg_ref[2] = sums["w0"]


def gram_outer(
    core_ref, first_ref, last_ref, in_ref, wg_ref, act_ref, high_ref, cot_ref,
    keep_ref, send_ref, taps, cots, out_ref, store,
):
    for index in range(4):
        zero_rows(taps, lane(index * RPAD))
        if index < 2:
            rows = rows_of(act_ref[index + 2])
        else:
            rows = turned(high_ref[index - 2], store.at[index - 2])
        fill_taps(taps, plane_at(index), rows)
    for slot in range(2):
        zero_rows(cots, lane(slot * RPAD))
    fill_rows(cots, plane_at(0), rows_of(cot_ref[PLANES - 1]))
    fill_rows(cots, plane_at(1), turned(high_ref[2], store.at[2]))

    def stay(index):
        return taps[:, pl.ds(plane_at(index), WIDTH)]

    five = (0, 1, 2, -1, -2)
    near = (-1, 0, 1)
    own = core_ref[0]
    first = first_ref[0].astype(f32)
    last = last_ref[0].astype(f32)

    def blocks(value, count):
        return [value[i * TAPS : (i + 1) * TAPS] for i in range(count)]

    def padded(value):
        return jnp.concatenate([value, jnp.zeros((value.shape[0], LANES - TAPS), f32)], 1)

    gap = jnp.zeros((LANES - TAPS, WIDTH), bf16)
    two, three = stay(0), stay(1)
    four = dot_nt(shifted(taps, 2, five), jnp.concatenate([three, gap, two, gap], 0))
    beyond = dot_nt(shifted(taps, 3, five), jnp.concatenate([three, gap], 0))
    x1 = blocks(four[:, :LANES], 5)
    x2 = blocks(four[:, LANES:] + beyond, 5)
    w_low = dot_nt(shifted(cots, 1, near), three)
    w_high = dot_nt(shifted(cots, 0, near), stay(2))

    def edge(left, right, row):
        return padded(dot_nt(
            taps[:, pl.ds(plane_at(left, row), LANES)], taps[:, pl.ds(plane_at(right, row), LANES)]
        ))

    wide = jnp.zeros((TAPS, LANES - TAPS), f32)
    wsums = (
        wg_ref[0] + jnp.concatenate([w_low, wide], 1),
        wg_ref[1],
        wg_ref[2] + jnp.concatenate([w_high, wide], 1),
    )
    at = lax.broadcasted_iota(jnp.int32, (TAPS, LANES), 1)

    def piece(t):
        if t > GRAD:
            return jnp.zeros((C, LANES), f32)
        if t == GRAD:
            return wsums[1][C : 2 * C]
        a, b, c = t // 9, t // 3 % 3, t % 3
        return pltpu.roll(wsums[a][(2 - b) * C : (3 - b) * C], TAPS - c * C, 1)

    def put(slot, value):
        extra = piece(slot)
        high = extra.astype(bf16).astype(f32)
        extra = jnp.concatenate([high, extra - high, jnp.zeros((C, LANES), f32)], 0)
        out_ref[(slot // HALF) ^ own, slot % HALF] = jnp.where(at < TAPS, value, extra).astype(bf16)

    def cut(value):
        return value

    for base, dx, parts, pairs in (
        (A_X1, 1, x1, ((2, 1),)),
        (A_X2, 2, x2, ((2, 0), (3, 1))),
    ):
        whole = cut(in_ref[base]) + parts[0]
        put(SLOT[(dx, "0")], whole)
        for j, (name, row) in enumerate((("f", 0), ("l", ROWS - 1))):
            edge_sum = cut(in_ref[base + 1 + j])
            for left, right in pairs:
                edge_sum = edge_sum + edge(left, right, row)
            put(SLOT[(dx, name)], whole - edge_sum)
        for j, dy in enumerate((1, 2, -1, -2)):
            put(SLOT[(dx, dy)], cut(in_ref[base + 3 + j]) + parts[1 + j])
    for name in ("0", "f", "l"):
        values = [cut(in_ref[A_X0 + i]) for i in range(5)]
        if name == "f":
            values = [v - first * cut(in_ref[A_P0 + i]) for i, v in enumerate(values)]
        if name == "l":
            values = [v - last * cut(in_ref[A_P3 + i]) for i, v in enumerate(values)]
        put(SLOT[(name, "0")], values[0])
        put(SLOT[(name, "f")], values[0] - values[1])
        put(SLOT[(name, "l")], values[0] - values[2])
        put(SLOT[(name, 1)], values[3])
        put(SLOT[(name, 2)], values[4])
    for slot in range(len(CLASSES), BLOCKS):
        put(slot, jnp.zeros((TAPS, LANES), f32))
    keep_ref[...] = out_ref[0]
    send_ref[...] = out_ref[1]


def settle(value):
    at = lax.broadcasted_iota(jnp.int32, (C, LANES), 1)
    first, second = value[:C], value[C : 2 * C]
    both = first + second
    high = both.astype(bf16).astype(f32)
    first = jnp.where(at < TAPS, first, high)
    second = jnp.where(at < TAPS, second, both - high)
    return jnp.concatenate([first, second, value[2 * C :]], 0).astype(bf16)


def add_kernel(keep_ref, arrived_ref, out_ref):
    for i in range(HALF):
        out_ref[i] = settle(keep_ref[i].astype(f32) + arrived_ref[i].astype(f32))


def sum_kernel(parts_ref, out_ref):
    total = parts_ref[0].astype(f32)
    for i in range(1, parts_ref.shape[0]):
        total = total + parts_ref[i].astype(f32)
    total = settle(total)
    for i in range(out_ref.shape[0]):
        out_ref[i] = total


def conv_kernel(which, x_ref, low_ref, high_ref, w_ref, out_ref, taps, store):
    for index in range(PLANES + 2):
        zero_rows(taps, lane(index * RPAD))
        if index == 0:
            rows = turned(low_ref[which], store.at[PLANES])
        elif index == PLANES + 1:
            rows = turned(high_ref[2 * which], store.at[PLANES + 1])
        else:
            rows = rows_of(x_ref[index - 1])
        fill_taps(taps, plane_at(index), rows)
    weight = w_ref[...]
    step = 2
    for x in range(PLANES):
        plane = store.at[x]
        for y in range(0, ROWS, step):
            patch = jnp.concatenate(
                [
                    taps[:, pl.ds(plane_at(x + 1 + dx, y + dy), step * LANES)]
                    for dx in (-1, 0, 1)
                    for dy in (-1, 0, 1)
                ],
                0,
            )
            value = jnp.dot(weight, patch, preferred_element_type=f32)
            for i in range(step):
                plane[(y + i) * C : (y + i + 1) * C, :] = value[:, lane(i) : lane(i + 1)]
        for channel in range(C):
            out_ref[channel, x] = plane[pl.ds(channel, ROWS, stride=C), :].astype(bf16)


def split(value):
    high = value.astype(bf16)
    return high, (value - high.astype(f32)).astype(bf16)


def class_of(offset):
    return {0: "0", 1: "f", -1: "l"}[offset]


def finish_kernel(core_ref, mine_ref, other_ref, out_ref, both, factor):
    own = core_ref[0]
    both[own] = mine_ref[...]
    both[1 - own] = other_ref[...]

    def block(slot):
        return both[slot // HALF, slot % HALF]

    at = lax.broadcasted_iota(jnp.int32, (TAPS, LANES), 1)
    offsets = [(a, b) for a in (-1, 0, 1) for b in (-1, 0, 1)]
    tail = jnp.zeros((LANES - TAPS, LANES), bf16)
    cache = {}

    def padded(slot):
        if slot not in cache:
            value = jnp.where(at < TAPS, block(slot), jnp.zeros((), bf16))
            full = jnp.concatenate([value, tail], 0)
            cache[slot] = (full, full.T)
        return cache[slot]

    for i, (ax, ay) in enumerate(offsets):
        for j, (bx, by) in enumerate(offsets):
            dx, dy = bx - ax, by - ay
            if dx < 0 or (dx == 0 and dy < 0):
                continue
            key = (class_of(ax) if dx == 0 else dx, class_of(ay) if dy == 0 else dy)
            full, turned = padded(SLOT[key])
            factor[lane(j) : lane(j + 1), lane(i) : lane(i + 1)] = full
            if i != j:
                factor[lane(i) : lane(i + 1), lane(j) : lane(j + 1)] = turned

    def extra(t):
        here = both.at[t // HALF, t % HALF]
        return here[0:C, :].astype(f32) + here[C : 2 * C, :].astype(f32)

    pieces = []
    for i in range(9):
        rows = jnp.zeros((C, LANES), f32)
        for c in range(3):
            moved = pltpu.roll(extra(3 * i + c), C + c * C, 1)
            rows = jnp.where(at[:C] // C == c, moved, rows)
        pieces.append(rows)
    wgrad = jnp.concatenate(pieces, 1) * (1.0 / CELLS)

    grad = extra(GRAD)[:, TAPS:LANES]
    row_id = lax.broadcasted_iota(jnp.int32, (C, C), 0)
    col_id = lax.broadcasted_iota(jnp.int32, (C, C), 1)
    eye = jnp.where(row_id == col_id, 1.0, 0.0).astype(f32)
    scaled = grad * (C / jnp.sum(grad * eye)) + DAMPING * eye
    bound = jnp.max(jnp.sum(jnp.abs(scaled), axis=1))
    inverse = eye / bound
    for _ in range(ITERS):
        half = jnp.dot(inverse, scaled, precision=lax.Precision.HIGHEST, preferred_element_type=f32)
        inverse = 2.0 * inverse - jnp.dot(
            half, inverse, precision=lax.Precision.HIGHEST, preferred_element_type=f32
        )

    trace = jnp.zeros((), f32)
    sums = jnp.zeros((1, WIDE), f32)
    diag_row = lax.broadcasted_iota(jnp.int32, (LANES, LANES), 0)
    diag_col = lax.broadcasted_iota(jnp.int32, (LANES, LANES), 1)
    diagonal = jnp.zeros((LANES, LANES), f32)
    for i in range(9):
        rows = factor[lane(i) : lane(i + 1), :].astype(f32)
        sums = sums + jnp.sum(jnp.abs(rows), axis=0, keepdims=True)
        diagonal = diagonal + jnp.where(diag_row == diag_col, rows[:, lane(i) : lane(i + 1)], 0.0)
    trace = jnp.sum(diagonal)
    scale = ORDER / trace
    bound = scale * jnp.max(sums) + DAMPING
    step = scale / bound
    keep = 1.0 - DAMPING / bound
    value = wgrad
    for _ in range(2**ITERS - 1):
        high, low = split(value)
        product = jnp.dot(jnp.concatenate([high, low], 0), factor[...], preferred_element_type=f32)
        value = wgrad + keep * value - step * (product[:C] + product[C:])
    right = value * (1.0 / bound)
    applied = jnp.dot(inverse, right, precision=lax.Precision.HIGHEST, preferred_element_type=f32)
    quadratic = jnp.sum(applied * wgrad)
    result = applied * jnp.sqrt(C * ORDER / quadratic)
    out_ref[...] = jnp.concatenate([result[:, lane(i) : lane(i) + TAPS] for i in range(9)], 1)


SMEM = pl.BlockSpec(memory_space=pltpu.SMEM)
WHOLE = pl.BlockSpec(memory_space=pltpu.VMEM)
IN_HBM = pl.BlockSpec(memory_space=pltpu.HBM)


def call(kernel, shapes, scratch, inputs, scalars=0, flops=0, mib=16, specs=None, out_specs=None):
    return pl.pallas_call(
        kernel,
        out_shape=shapes,
        in_specs=specs or [SMEM] * scalars + [WHOLE] * (len(inputs) - scalars),
        out_specs=out_specs or jax.tree.map(lambda _: WHOLE, shapes),
        scratch_shapes=scratch,
        compiler_params=pltpu.CompilerParams(vmem_limit_bytes=mib * MIB),
        cost_estimate=pl.CostEstimate(flops=flops, bytes_accessed=1 << 20, transcendentals=0),
    )(*inputs)


def edge_kernel(act, cot, down_out, up_out, down, up, sems):
    hops = []
    for k, (source, plane, buffer, target, slot) in enumerate((
        (act, 0, down, down_out, 0),
        (act, 1, down, down_out, 1),
        (cot, 0, down, down_out, 2),
        (act, PLANES - 1, up, up_out, 0),
        (cot, PLANES - 1, up, up_out, 1),
    )):
        hops.append((
            pltpu.make_async_copy(source.at[:, plane], buffer.at[slot], sems.at[2 * k]),
            pltpu.make_async_copy(buffer.at[slot], target.at[slot], sems.at[2 * k + 1]),
        ))
    for fetch, _ in hops:
        fetch.start()
    for fetch, put in hops:
        fetch.wait()
        put.start()
    for _, put in hops:
        put.wait()


def edge_planes(act, cot):
    down, up = (3, C, ROWS, LANES), (2, C, ROWS, LANES)
    return call(
        edge_kernel,
        (pltpu.HBM(down, bf16), pltpu.HBM(up, bf16)),
        [pltpu.VMEM(down, bf16), pltpu.VMEM(up, bf16), pltpu.SemaphoreType.DMA((10,))],
        (act, cot),
        mib=4,
        specs=[IN_HBM] * 2,
        out_specs=(IN_HBM, IN_HBM),
    )


def conv(which, planes, low, high, weight):
    return call(
        functools.partial(conv_kernel, which),
        jax.ShapeDtypeStruct((C, PLANES, ROWS, LANES), bf16),
        [
            pltpu.VMEM((TAPS, 6 * RPAD * LANES), bf16),
            pltpu.VMEM((PLANES + 2, C * ROWS, LANES), f32),
        ],
        (planes, low, high, weight),
        flops=2 * C * ORDER * PLANES * ROWS * LANES,
        mib=12,
    )


def body(activations, cotangent, weight):
    space = ("y", "x", "z_lo")
    size = lax.axis_size(space)
    up = [(i, i + 1) for i in range(size - 1)]
    down = [(j, i) for i, j in up]
    hold = lax.optimization_barrier

    act = pltpu.with_memory_space_constraint(activations[0], pltpu.HBM)
    cot = pltpu.with_memory_space_constraint(cotangent[0], pltpu.HBM)
    for_below, for_above = edge_planes(act, cot)
    high = lax.ppermute(for_below, space, down)
    where = lax.axis_index(space)
    core = lax.axis_index("core").astype(jnp.int32).reshape(1)
    first = (where == 0).astype(jnp.int32).reshape(1)
    last = (where == size - 1).astype(jnp.int32).reshape(1)

    turned_shape = pltpu.VMEM((PLANES, ROWS, C, LANES), bf16)
    sums, wsums, turned_act, turned_cot = call(
        gram_inner,
        (
            pltpu.VMEM((A_BLOCKS, TAPS, LANES), f32),
            pltpu.VMEM((3, TAPS, LANES), f32),
            turned_shape,
            turned_shape,
        ),
        [
            pltpu.VMEM((TAPS, PLANES * RPAD * LANES), bf16),
            pltpu.VMEM((C, PLANES * RPAD * LANES), bf16),
            pltpu.VMEM((2 * PLANES, C * ROWS, LANES), f32),
            pltpu.VMEM((PLANES, C, ROWS, LANES), bf16),
            pltpu.VMEM((PLANES, C, ROWS, LANES), bf16),
            pltpu.SemaphoreType.DMA((2 * PLANES,)),
        ],
        (act, cot),
        specs=[IN_HBM] * 2,
        flops=24 * 10**9 // 4,
        mib=MIB_INNER,
    )
    for_above, sums, wsums = hold((for_above, sums, wsums))
    low = lax.ppermute(for_above, space, up)
    blocks_half = jax.ShapeDtypeStruct((HALF, TAPS, LANES), bf16)
    keep, send = call(
        gram_outer,
        (blocks_half, blocks_half),
        [
            pltpu.VMEM((TAPS, 4 * RPAD * LANES), bf16),
            pltpu.VMEM((C, 2 * RPAD * LANES), bf16),
            pltpu.VMEM((2, HALF, TAPS, LANES), bf16),
            pltpu.VMEM((3, C * ROWS, LANES), f32),
        ],
        (core, first, last, sums, wsums, turned_act, high, turned_cot),
        scalars=3,
        flops=10**9,
        mib=MIB_OUTER,
    )

    swap = [(0, 1), (1, 0)]
    arrived = lax.ppermute(send, "core", swap)
    mine = call(add_kernel, blocks_half, [], (keep, arrived), mib=4)
    parts = lax.all_to_all(mine, ("y", "x"), 0, 0, tiled=True)
    depth = lax.axis_size(("z_hi", "z_lo"))
    block = call(sum_kernel, jax.ShapeDtypeStruct((depth, TAPS, LANES), bf16), [], (parts,), mib=4)
    block, act, cot, high, weight = hold((block, turned_act, turned_cot, high, weight))
    parts = lax.all_to_all(block, ("z_hi", "z_lo"), 0, 0, tiled=True)
    out = conv(0, act, low, high, weight)
    flipped = weight.reshape(C, 27, C)[:, ::-1, :].transpose(2, 1, 0).reshape(C, ORDER)
    back = conv(1, cot, low, high, flipped)
    parts, out, back = hold((parts, out, back))
    block = call(sum_kernel, blocks_half, [], (parts,), mib=4)
    whole = lax.all_to_all(block, ("y", "x"), 0, 0, tiled=True)
    other = lax.ppermute(whole, "core", swap)
    precond = call(
        finish_kernel,
        jax.ShapeDtypeStruct((C, ORDER), f32),
        [pltpu.VMEM((2, HALF, TAPS, LANES), bf16), pltpu.VMEM((WIDE, WIDE), bf16)],
        (core, whole, other),
        scalars=1,
        flops=10**9,
    )
    return out[None], back[None], precond


def solution(mesh):
    fine = Mesh(mesh.devices.reshape(2, 2, 4, 4, 4), ("z_hi", "core", "y", "x", "z_lo"))
    spec = P(("z_hi", "core"), None, ("y", "x", "z_lo"), None, None)
    return jax.shard_map(
        body,
        mesh=fine,
        in_specs=(spec, spec, P()),
        out_specs=(spec, spec, P()),
        check_vma=False,
    )
```

```python
import functools

import jax
import jax.numpy as jnp
from jax import lax
from jax.experimental import pallas as pl
from jax.experimental.pallas import tpu as pltpu
from jax.sharding import Mesh
from jax.sharding import PartitionSpec as P

ITERS = 3
DAMPING = 0.1
C = 32
PLANES = 4
ROWS = 16
LANES = 128
RPAD = ROWS + 4
TAPS = 3 * C
ORDER = 27 * C
WIDE = 9 * LANES
CELLS = 2097152
MIB = 1024 * 1024
MIB_INNER, MIB_OUTER = 16, 16
NT = (((1,), (1,)), ((), ()))
f32 = jnp.float32
bf16 = jnp.bfloat16


CLASSES = []
for _x in ("0", "f", "l"):
    for _y in ("0", "f", "l", 1, 2):
        CLASSES.append((_x, _y))
for _x in (1, 2):
    for _y in ("0", "f", "l", 1, 2, -1, -2):
        CLASSES.append((_x, _y))
SLOT = {key: index for index, key in enumerate(CLASSES)}
GRAD = 27
BLOCKS = 32
HALF = BLOCKS // 2


def lane(row):
    return row * LANES


def turned(plane, store):
    store[...] = plane.astype(f32).reshape(C * ROWS, LANES)
    return [store[pl.ds(y, C, stride=ROWS), :] for y in range(ROWS)]


def rows_of(plane):
    return [plane[y].astype(f32) for y in range(ROWS)]


def fill_taps(dst, col, rows):
    at = lax.broadcasted_iota(jnp.int32, (C, LANES), 1)
    for y in range(ROWS):
        here = pl.ds(col + lane(y), LANES)
        before = jnp.where(at == 0, 0.0, pltpu.roll(rows[y], 1, 1))
        after = jnp.where(at == LANES - 1, 0.0, pltpu.roll(rows[y], LANES - 1, 1))
        dst[0:C, here] = before.astype(bf16)
        dst[C : 2 * C, here] = rows[y].astype(bf16)
        dst[2 * C : 3 * C, here] = after.astype(bf16)


def fill_rows(dst, col, rows):
    for y in range(ROWS):
        dst[:, pl.ds(col + lane(y), LANES)] = rows[y].astype(bf16)


def zero_rows(dst, col):
    zero = jnp.zeros((dst.shape[0], 2 * LANES), dst.dtype)
    dst[:, pl.ds(col, 2 * LANES)] = zero
    dst[:, pl.ds(col + lane(ROWS + 2), 2 * LANES)] = zero


def plane_at(index, row=0):
    return lane(index * RPAD + 2 + row)


def dot_nt(left, right):
    return lax.dot_general(left, right, NT, preferred_element_type=f32)


WIDTH = ROWS * LANES


def shifted(ref, index, rows, width=WIDTH):
    return jnp.concatenate([ref[:, pl.ds(plane_at(index, dy), width)] for dy in rows], 0)


A_P0, A_P3, A_X0 = 0, 5, 10
A_X1, A_X2 = 15, 22
A_BLOCKS = 29


def flip_taps(w_ref, flipped_ref):
    wide = jnp.concatenate([w_ref[...].astype(f32), jnp.zeros((C, 7 * LANES - ORDER), f32)], 1)
    tall = jnp.concatenate([wide, jnp.zeros((LANES - C, 7 * LANES), f32)], 0).T
    for group in range(7):
        total = jnp.zeros((C, LANES), f32)
        for place in range(4):
            tap = 26 - 4 * group - place
            if tap >= 0:
                block = tall[tap * C : (tap + 1) * C, :]
                total = total + (pltpu.roll(block, place * C, 1) if place else block)
        width = min(LANES, ORDER - lane(group))
        flipped_ref[:, lane(group) : lane(group) + width] = total[:, :width].astype(bf16)


def gram_inner(
    act_hbm, cot_hbm, w_ref, out_ref, wg_ref, turned_act, turned_cot, flipped_ref, above_ref,
    taps, cots, store, act_ref, cot_ref, sems,
):
    fetches = []
    for x in range(PLANES):
        for i, (source, target) in enumerate(((act_hbm, act_ref), (cot_hbm, cot_ref))):
            fetches.append(
                pltpu.make_async_copy(source.at[:, x], target.at[x], sems.at[2 * x + i])
            )
    for fetch in fetches:
        fetch.start()
    flip_taps(w_ref, flipped_ref)
    for x in range(PLANES):
        zero_rows(taps, lane(x * RPAD))
        zero_rows(cots, lane(x * RPAD))
    for x in range(PLANES):
        fetches[2 * x].wait()
        fetches[2 * x + 1].wait()
        rows = turned(act_ref[x], store.at[2 * x])
        fill_taps(taps, plane_at(x), rows)
        cot_rows = turned(cot_ref[x], store.at[2 * x + 1])
        fill_rows(cots, plane_at(x), cot_rows)
        if x == PLANES - 1:
            above_ref[0] = act_ref[x]
            above_ref[1] = cot_ref[x]
        for y in range(ROWS):
            turned_act[x, y] = rows[y].astype(bf16)
            turned_cot[x, y] = cot_rows[y].astype(bf16)

    def put(slot, value):
        out_ref[slot] = value

    def blocks(value, count):
        return [value[i * TAPS : (i + 1) * TAPS] for i in range(count)]

    near = (-1, 0, 1)
    sums = {}

    def add(key, value):
        sums[key] = value if key not in sums else sums[key] + value

    for x in range(PLANES):
        stay = jnp.concatenate(
            [taps[:, pl.ds(plane_at(x), WIDTH)], cots[:, pl.ds(plane_at(x), WIDTH)]], 0
        )
        level = dot_nt(shifted(taps, x, (0, 1, 2)), stay)
        zero, one, two = blocks(level, 3)
        cot_rows = [dot_nt(shifted(cots, x, near), stay)]
        if x + 1 < PLANES:
            up = dot_nt(shifted(taps, x + 1, (0, 1, 2, -1, -2)), stay)
            add("x1", up)
            cot_rows.append(dot_nt(shifted(cots, x + 1, near), stay))
            add("w2", cot_rows[1])
        if x >= 1:
            add("w0", dot_nt(shifted(cots, x - 1, near), stay))
        add("w1", cot_rows[0])
        if x + 2 < PLANES:
            add("x2", dot_nt(shifted(taps, x + 2, (0, 1, 2, -1, -2)), stay))
        edge = {}
        for name, row in (("F", 0), ("L", ROWS - 1)):
            stay_row = taps[:, pl.ds(plane_at(x, row), LANES)]
            count = min(3, PLANES - x)
            moving = jnp.concatenate(
                [taps[:, pl.ds(plane_at(x + i, row), LANES)] for i in range(count)], 0
            )
            edge_sum = blocks(jnp.pad(dot_nt(moving, stay_row), ((0, 0), (0, C))), count)
            edge[name] = edge_sum[0]
            for i in range(1, count):
                add((name, i), edge_sum[i])
        for i, value in enumerate((zero, edge["F"], edge["L"], one, two)):
            add(("level", i), value)
            if x == 0:
                put(A_P0 + i, value)
            if x == PLANES - 1:
                put(A_P3 + i, value)
    for i in range(5):
        put(A_X0 + i, sums[("level", i)])
    for base, name, i in ((A_X1, "x1", 1), (A_X2, "x2", 2)):
        whole = blocks(sums[name], 5)
        for j, value in enumerate((whole[0], sums[("F", i)], sums[("L", i)], *whole[1:])):
            put(base + j, value)
    wg_ref[0] = sums["w2"]
    wg_ref[1] = sums["w1"]
    wg_ref[2] = sums["w0"]


def gram_outer(
    core_ref, first_ref, last_ref, in_ref, wg_ref, act_ref, high_ref, cot_ref,
    keep_ref, send_ref, taps, cots, out_ref, store,
):
    for index in range(4):
        zero_rows(taps, lane(index * RPAD))
        if index < 2:
            rows = rows_of(act_ref[index + 2])
        else:
            rows = turned(high_ref[index - 2], store.at[index - 2])
        fill_taps(taps, plane_at(index), rows)
    for slot in range(2):
        zero_rows(cots, lane(slot * RPAD))
    fill_rows(cots, plane_at(0), rows_of(cot_ref[PLANES - 1]))
    fill_rows(cots, plane_at(1), turned(high_ref[2], store.at[2]))

    def stay(index):
        return taps[:, pl.ds(plane_at(index), WIDTH)]

    five = (0, 1, 2, -1, -2)
    near = (-1, 0, 1)
    own = core_ref[0]
    first = first_ref[0].astype(f32)
    last = last_ref[0].astype(f32)

    def blocks(value, count):
        return [value[i * TAPS : (i + 1) * TAPS] for i in range(count)]

    def padded(value):
        return jnp.concatenate([value, jnp.zeros((value.shape[0], LANES - TAPS), f32)], 1)

    gap = jnp.zeros((LANES - TAPS, WIDTH), bf16)
    two, three = stay(0), stay(1)
    four = dot_nt(shifted(taps, 2, five), jnp.concatenate([three, gap, two, gap], 0))
    beyond = dot_nt(shifted(taps, 3, five), jnp.concatenate([three, gap], 0))
    x1 = blocks(four[:, :LANES], 5)
    x2 = blocks(four[:, LANES:] + beyond, 5)
    w_low = dot_nt(shifted(cots, 1, near), three)
    w_high = dot_nt(shifted(cots, 0, near), stay(2))

    def edge(left, right, row):
        return padded(dot_nt(
            taps[:, pl.ds(plane_at(left, row), LANES)], taps[:, pl.ds(plane_at(right, row), LANES)]
        ))

    wide = jnp.zeros((TAPS, LANES - TAPS), f32)
    wsums = (
        wg_ref[0] + jnp.concatenate([w_low, wide], 1),
        wg_ref[1],
        wg_ref[2] + jnp.concatenate([w_high, wide], 1),
    )
    at = lax.broadcasted_iota(jnp.int32, (TAPS, LANES), 1)

    def piece(t):
        if t > GRAD:
            return jnp.zeros((C, LANES), f32)
        if t == GRAD:
            return wsums[1][C : 2 * C]
        a, b, c = t // 9, t // 3 % 3, t % 3
        return pltpu.roll(wsums[a][(2 - b) * C : (3 - b) * C], TAPS - c * C, 1)

    def put(slot, value):
        extra = piece(slot)
        high = extra.astype(bf16).astype(f32)
        extra = jnp.concatenate([high, extra - high, jnp.zeros((C, LANES), f32)], 0)
        out_ref[(slot // HALF) ^ own, slot % HALF] = jnp.where(at < TAPS, value, extra).astype(bf16)

    def cut(value):
        return value

    for base, dx, parts, pairs in (
        (A_X1, 1, x1, ((2, 1),)),
        (A_X2, 2, x2, ((2, 0), (3, 1))),
    ):
        whole = cut(in_ref[base]) + parts[0]
        put(SLOT[(dx, "0")], whole)
        for j, (name, row) in enumerate((("f", 0), ("l", ROWS - 1))):
            edge_sum = cut(in_ref[base + 1 + j])
            for left, right in pairs:
                edge_sum = edge_sum + edge(left, right, row)
            put(SLOT[(dx, name)], whole - edge_sum)
        for j, dy in enumerate((1, 2, -1, -2)):
            put(SLOT[(dx, dy)], cut(in_ref[base + 3 + j]) + parts[1 + j])
    for name in ("0", "f", "l"):
        values = [cut(in_ref[A_X0 + i]) for i in range(5)]
        if name == "f":
            values = [v - first * cut(in_ref[A_P0 + i]) for i, v in enumerate(values)]
        if name == "l":
            values = [v - last * cut(in_ref[A_P3 + i]) for i, v in enumerate(values)]
        put(SLOT[(name, "0")], values[0])
        put(SLOT[(name, "f")], values[0] - values[1])
        put(SLOT[(name, "l")], values[0] - values[2])
        put(SLOT[(name, 1)], values[3])
        put(SLOT[(name, 2)], values[4])
    for slot in range(len(CLASSES), BLOCKS):
        put(slot, jnp.zeros((TAPS, LANES), f32))
    keep_ref[...] = out_ref[0]
    send_ref[...] = out_ref[1]


def settle(value):
    at = lax.broadcasted_iota(jnp.int32, (C, LANES), 1)
    first, second = value[:C], value[C : 2 * C]
    both = first + second
    high = both.astype(bf16).astype(f32)
    first = jnp.where(at < TAPS, first, high)
    second = jnp.where(at < TAPS, second, both - high)
    return jnp.concatenate([first, second, value[2 * C :]], 0).astype(bf16)


def add_kernel(keep_ref, arrived_ref, out_ref):
    for i in range(HALF):
        out_ref[i] = settle(keep_ref[i].astype(f32) + arrived_ref[i].astype(f32))


def sum_kernel(parts_ref, out_ref):
    total = parts_ref[0].astype(f32)
    for i in range(1, parts_ref.shape[0]):
        total = total + parts_ref[i].astype(f32)
    total = settle(total)
    for i in range(out_ref.shape[0]):
        out_ref[i] = total


def conv_kernel(
    act_ref, cot_ref, low_ref, high_ref, w_ref, flipped_ref, out_ref, back_ref,
    act_taps, cot_taps, store, halos,
):
    step = 2

    def fill(which, index):
        planes, dst = ((act_ref, act_taps), (cot_ref, cot_taps))[which]
        zero_rows(dst, lane(index * RPAD))
        if index == 0:
            rows = turned(low_ref[which], halos.at[which, 0])
        elif index == PLANES + 1:
            rows = turned(high_ref[2 * which], halos.at[which, 1])
        else:
            rows = rows_of(planes[index - 1])
        fill_taps(dst, plane_at(index), rows)

    def products(which, x, weight):
        src = (act_taps, cot_taps)[which]
        plane = store.at[which, x]
        for y in range(0, ROWS, step):
            patch = jnp.concatenate(
                [
                    src[:, pl.ds(plane_at(x + 1 + dx, y + dy), step * LANES)]
                    for dx in (-1, 0, 1)
                    for dy in (-1, 0, 1)
                ],
                0,
            )
            value = jnp.dot(weight, patch, preferred_element_type=f32)
            for i in range(step):
                plane[(y + i) * C : (y + i + 1) * C, :] = value[:, lane(i) : lane(i + 1)]

    def put(which, x):
        target = (out_ref, back_ref)[which]
        for channel in range(C):
            target[channel, x] = store[which, x, pl.ds(channel, ROWS, stride=C), :].astype(bf16)

    weights = (w_ref[...], flipped_ref[...])
    fills = [(which, index) for which in (0, 1) for index in range(PLANES + 2)]
    for _ in range(3):
        fill(*fills.pop(0))
    before = None
    for which in (0, 1):
        for x in range(PLANES):
            products(which, x, weights[which])
            for _ in range(2 if which == 0 and x < 3 else 1):
                if fills:
                    fill(*fills.pop(0))
            if before:
                put(*before)
            before = (which, x)
    put(*before)


def split(value):
    high = value.astype(bf16)
    return high, (value - high.astype(f32)).astype(bf16)


def class_of(offset):
    return {0: "0", 1: "f", -1: "l"}[offset]


def finish_kernel(core_ref, mine_ref, other_ref, out_ref, factor):
    own = core_ref[0]

    def chosen(slot, rows=slice(None)):
        here = own == slot // HALF
        return jnp.where(here, mine_ref[slot % HALF, rows, :], other_ref[slot % HALF, rows, :])

    at = lax.broadcasted_iota(jnp.int32, (TAPS, LANES), 1)
    offsets = [(a, b) for a in (-1, 0, 1) for b in (-1, 0, 1)]
    tail = jnp.zeros((LANES - TAPS, LANES), f32)
    diag_row = lax.broadcasted_iota(jnp.int32, (LANES, LANES), 0)
    diag_col = lax.broadcasted_iota(jnp.int32, (LANES, LANES), 1)
    cache = {}

    def size(value):
        return jnp.sum(jnp.abs(value), axis=0, keepdims=True)

    def padded(slot, symmetric):
        if slot not in cache:
            value = jnp.where(at < TAPS, chosen(slot).astype(f32), 0.0)
            full = jnp.concatenate([value, tail], 0)
            turned = full if symmetric else full.T
            cache[slot] = (full.astype(bf16), turned.astype(bf16), size(full), size(turned), full)
        return cache[slot]

    sums = [jnp.zeros((1, LANES), f32) for _ in offsets]
    diagonal = jnp.zeros((LANES, LANES), f32)
    for i, (ax, ay) in enumerate(offsets):
        for j, (bx, by) in enumerate(offsets):
            dx, dy = bx - ax, by - ay
            if dx < 0 or (dx == 0 and dy < 0):
                continue
            key = (class_of(ax) if dx == 0 else dx, class_of(ay) if dy == 0 else dy)
            full, turned, size_full, size_turned, wide = padded(SLOT[key], i == j)
            factor[lane(j) : lane(j + 1), lane(i) : lane(i + 1)] = full
            sums[i] = sums[i] + size_full
            if i != j:
                factor[lane(i) : lane(i + 1), lane(j) : lane(j + 1)] = turned
                sums[j] = sums[j] + size_turned
            else:
                diagonal = diagonal + jnp.where(diag_row == diag_col, wide, 0.0)

    def extra(t):
        return chosen(t, slice(0, C)).astype(f32) + chosen(t, slice(C, 2 * C)).astype(f32)

    pieces = []
    for i in range(9):
        rows = jnp.zeros((C, LANES), f32)
        for c in range(3):
            moved = pltpu.roll(extra(3 * i + c), C + c * C, 1)
            rows = jnp.where(at[:C] // C == c, moved, rows)
        pieces.append(rows)
    wgrad = jnp.concatenate(pieces, 1) * (1.0 / CELLS)

    def exact(left, right):
        return jnp.dot(left, right, precision=lax.Precision.HIGHEST, preferred_element_type=f32)

    grad = extra(GRAD)[:, TAPS:LANES]
    row_id = lax.broadcasted_iota(jnp.int32, (C, C), 0)
    col_id = lax.broadcasted_iota(jnp.int32, (C, C), 1)
    eye = jnp.where(row_id == col_id, 1.0, 0.0).astype(f32)
    scaled = grad * (C / jnp.sum(grad * eye)) + DAMPING * eye
    inverse = eye / jnp.max(jnp.sum(jnp.abs(scaled), axis=1))

    scale = ORDER / jnp.sum(diagonal)
    bound = scale * jnp.max(jnp.concatenate(sums, 0)) + DAMPING
    step = scale / bound
    keep = 1.0 - DAMPING / bound
    value = wgrad
    half = None
    for sweep in range(2**ITERS - 1):
        high, low = split(value)
        product = jnp.dot(jnp.concatenate([high, low], 0), factor[...], preferred_element_type=f32)
        if sweep < 2 * ITERS:
            if sweep % 2 == 0:
                half = exact(inverse, scaled)
            else:
                inverse = 2.0 * inverse - exact(half, inverse)
        value = wgrad + keep * value - step * (product[:C] + product[C:])
    right = value * (1.0 / bound)
    applied = exact(inverse, right)
    quadratic = jnp.sum(applied * wgrad)
    result = applied * jnp.sqrt(C * ORDER / quadratic)
    out_ref[...] = jnp.concatenate([result[:, lane(i) : lane(i) + TAPS] for i in range(9)], 1)


SMEM = pl.BlockSpec(memory_space=pltpu.SMEM)
WHOLE = pl.BlockSpec(memory_space=pltpu.VMEM)
IN_HBM = pl.BlockSpec(memory_space=pltpu.HBM)


def call(kernel, shapes, scratch, inputs, scalars=0, flops=0, mib=16, specs=None, out_specs=None):
    return pl.pallas_call(
        kernel,
        out_shape=shapes,
        in_specs=specs or [SMEM] * scalars + [WHOLE] * (len(inputs) - scalars),
        out_specs=out_specs or jax.tree.map(lambda _: WHOLE, shapes),
        scratch_shapes=scratch,
        compiler_params=pltpu.CompilerParams(vmem_limit_bytes=mib * MIB),
        cost_estimate=pl.CostEstimate(flops=flops, bytes_accessed=1 << 20, transcendentals=0),
    )(*inputs)


def edge_kernel(act, cot, down, sems):
    copies = [
        pltpu.make_async_copy(source.at[:, plane], down.at[k], sems.at[k])
        for k, (source, plane) in enumerate(((act, 0), (act, 1), (cot, 0)))
    ]
    for copy in copies:
        copy.start()
    for copy in copies:
        copy.wait()


def edge_planes(act, cot):
    return call(
        edge_kernel,
        pltpu.VMEM((3, C, ROWS, LANES), bf16),
        [pltpu.SemaphoreType.DMA((3,))],
        (act, cot),
        mib=4,
        specs=[IN_HBM] * 2,
    )


def conv(act, cot, low, high, weight, flipped):
    taps = pltpu.VMEM((TAPS, 6 * RPAD * LANES), bf16)
    shape = jax.ShapeDtypeStruct((C, PLANES, ROWS, LANES), bf16)
    return call(
        conv_kernel,
        (shape, shape),
        [
            taps,
            taps,
            pltpu.VMEM((2, PLANES, C * ROWS, LANES), f32),
            pltpu.VMEM((2, 2, C * ROWS, LANES), f32),
        ],
        (act, cot, low, high, weight, flipped),
        flops=4 * C * ORDER * PLANES * ROWS * LANES,
        mib=20,
    )


def body(activations, cotangent, weight):
    space = ("y", "x", "z_lo")
    size = lax.axis_size(space)
    up = [(i, i + 1) for i in range(size - 1)]
    down = [(j, i) for i, j in up]
    hold = lax.optimization_barrier

    act = pltpu.with_memory_space_constraint(activations[0], pltpu.HBM)
    cot = pltpu.with_memory_space_constraint(cotangent[0], pltpu.HBM)
    for_below = edge_planes(act, cot)
    high = lax.ppermute(for_below, space, down)
    where = lax.axis_index(space)
    core = lax.axis_index("core").astype(jnp.int32).reshape(1)
    first = (where == 0).astype(jnp.int32).reshape(1)
    last = (where == size - 1).astype(jnp.int32).reshape(1)

    turned_shape = pltpu.VMEM((PLANES, ROWS, C, LANES), bf16)
    sums, wsums, turned_act, turned_cot, flipped, for_above = call(
        gram_inner,
        (
            pltpu.VMEM((A_BLOCKS, TAPS, LANES), f32),
            pltpu.VMEM((3, TAPS, LANES), f32),
            turned_shape,
            turned_shape,
            jax.ShapeDtypeStruct((C, ORDER), bf16),
            jax.ShapeDtypeStruct((2, C, ROWS, LANES), bf16),
        ),
        [
            pltpu.VMEM((TAPS, PLANES * RPAD * LANES), bf16),
            pltpu.VMEM((C, PLANES * RPAD * LANES), bf16),
            pltpu.VMEM((2 * PLANES, C * ROWS, LANES), f32),
            pltpu.VMEM((PLANES, C, ROWS, LANES), bf16),
            pltpu.VMEM((PLANES, C, ROWS, LANES), bf16),
            pltpu.SemaphoreType.DMA((2 * PLANES,)),
        ],
        (act, cot, weight),
        specs=[IN_HBM, IN_HBM, WHOLE],
        flops=24 * 10**9 // 4,
        mib=MIB_INNER,
    )
    for_above, sums, wsums = hold((for_above, sums, wsums))
    low = lax.ppermute(for_above, space, up)
    blocks_half = jax.ShapeDtypeStruct((HALF, TAPS, LANES), bf16)
    keep, send = call(
        gram_outer,
        (blocks_half, blocks_half),
        [
            pltpu.VMEM((TAPS, 4 * RPAD * LANES), bf16),
            pltpu.VMEM((C, 2 * RPAD * LANES), bf16),
            pltpu.VMEM((2, HALF, TAPS, LANES), bf16),
            pltpu.VMEM((3, C * ROWS, LANES), f32),
        ],
        (core, first, last, sums, wsums, turned_act, high, turned_cot),
        scalars=3,
        flops=10**9,
        mib=MIB_OUTER,
    )

    swap = [(0, 1), (1, 0)]
    arrived = lax.ppermute(send, "core", swap)
    mine = call(add_kernel, blocks_half, [], (keep, arrived), mib=4)
    parts = lax.all_to_all(mine, ("y", "x"), 0, 0, tiled=True)
    depth = lax.axis_size(("z_hi", "z_lo"))
    block = call(sum_kernel, jax.ShapeDtypeStruct((depth, TAPS, LANES), bf16), [], (parts,), mib=4)
    block, act, cot, high, weight = hold((block, turned_act, turned_cot, high, weight))
    parts = lax.all_to_all(block, ("z_hi", "z_lo"), 0, 0, tiled=True)
    out, back = conv(act, cot, low, high, weight, flipped)
    parts, out, back = hold((parts, out, back))
    block = call(sum_kernel, blocks_half, [], (parts,), mib=4)
    whole = lax.all_to_all(block, ("y", "x"), 0, 0, tiled=True)
    other = lax.ppermute(whole, "core", swap)
    precond = call(
        finish_kernel,
        jax.ShapeDtypeStruct((C, ORDER), f32),
        [pltpu.VMEM((WIDE, WIDE), bf16)],
        (core, whole, other),
        scalars=1,
        flops=10**9,
    )
    return out[None], back[None], precond


def solution(mesh):
    fine = Mesh(mesh.devices.reshape(2, 2, 4, 4, 4), ("z_hi", "core", "y", "x", "z_lo"))
    spec = P(("z_hi", "core"), None, ("y", "x", "z_lo"), None, None)
    return jax.shard_map(
        body,
        mesh=fine,
        in_specs=(spec, spec, P()),
        out_specs=(spec, spec, P()),
        check_vma=False,
    )
```

```python
import functools

import jax
import jax.numpy as jnp
from jax import lax
from jax.experimental import pallas as pl
from jax.experimental.pallas import tpu as pltpu
from jax.sharding import Mesh
from jax.sharding import PartitionSpec as P

ITERS = 3
DAMPING = 0.1
C = 32
PLANES = 4
ROWS = 16
LANES = 128
RPAD = ROWS + 4
TAPS = 3 * C
ORDER = 27 * C
WIDE = 9 * LANES
CELLS = 2097152
MIB = 1024 * 1024
MIB_INNER, MIB_OUTER = 16, 16
NT = (((1,), (1,)), ((), ()))
f32 = jnp.float32
bf16 = jnp.bfloat16


CLASSES = []
for _x in ("0", "f", "l"):
    for _y in ("0", "f", "l", 1, 2):
        CLASSES.append((_x, _y))
for _x in (1, 2):
    for _y in ("0", "f", "l", 1, 2, -1, -2):
        CLASSES.append((_x, _y))
SLOT = {key: index for index, key in enumerate(CLASSES)}
GRAD = 27
BLOCKS = 32
HALF = BLOCKS // 2


def lane(row):
    return row * LANES


def turned(plane, store):
    store[...] = plane.astype(f32).reshape(C * ROWS, LANES)
    return [store[pl.ds(y, C, stride=ROWS), :] for y in range(ROWS)]


def halo_planes(odd, one_ref, two_ref):
    one, two = one_ref[...].astype(f32), two_ref[...].astype(f32)
    return jnp.where(odd, two, one), jnp.where(odd, one, two)


def rows_of(plane):
    return [plane[y].astype(f32) for y in range(ROWS)]


def fill_taps(dst, col, rows):
    at = lax.broadcasted_iota(jnp.int32, (C, LANES), 1)
    for y in range(ROWS):
        here = pl.ds(col + lane(y), LANES)
        before = jnp.where(at == 0, 0.0, pltpu.roll(rows[y], 1, 1))
        after = jnp.where(at == LANES - 1, 0.0, pltpu.roll(rows[y], LANES - 1, 1))
        dst[0:C, here] = before.astype(bf16)
        dst[C : 2 * C, here] = rows[y].astype(bf16)
        dst[2 * C : 3 * C, here] = after.astype(bf16)


def fill_rows(dst, col, rows):
    for y in range(ROWS):
        dst[:, pl.ds(col + lane(y), LANES)] = rows[y].astype(bf16)


def zero_rows(dst, col):
    zero = jnp.zeros((dst.shape[0], 2 * LANES), dst.dtype)
    dst[:, pl.ds(col, 2 * LANES)] = zero
    dst[:, pl.ds(col + lane(ROWS + 2), 2 * LANES)] = zero


def plane_at(index, row=0):
    return lane(index * RPAD + 2 + row)


def dot_nt(left, right):
    return lax.dot_general(left, right, NT, preferred_element_type=f32)


WIDTH = ROWS * LANES


def shifted(ref, index, rows, width=WIDTH):
    return jnp.concatenate([ref[:, pl.ds(plane_at(index, dy), width)] for dy in rows], 0)


A_P0, A_P3, A_X0 = 0, 5, 10
A_X1, A_X2 = 15, 22
A_BLOCKS = 29


def flip_taps(w_ref, flipped_ref):
    wide = jnp.concatenate([w_ref[...].astype(f32), jnp.zeros((C, 7 * LANES - ORDER), f32)], 1)
    tall = jnp.concatenate([wide, jnp.zeros((LANES - C, 7 * LANES), f32)], 0).T
    for group in range(7):
        total = jnp.zeros((C, LANES), f32)
        for place in range(4):
            tap = 26 - 4 * group - place
            if tap >= 0:
                block = tall[tap * C : (tap + 1) * C, :]
                total = total + (pltpu.roll(block, place * C, 1) if place else block)
        width = min(LANES, ORDER - lane(group))
        flipped_ref[:, lane(group) : lane(group) + width] = total[:, :width].astype(bf16)


def gram_inner(
    odd_ref, act_hbm, cot_hbm, w_ref,
    out_ref, wg_ref, turned_act, turned_cot, flipped_ref, one_ref, two_ref,
    taps, cots, store, act_ref, cot_ref, sems,
):
    fetches = []
    for x in range(PLANES):
        for i, (source, target) in enumerate(((act_hbm, act_ref), (cot_hbm, cot_ref))):
            fetches.append(
                pltpu.make_async_copy(source.at[:, x], target.at[x], sems.at[2 * x + i])
            )
    for fetch in fetches:
        fetch.start()
    flip_taps(w_ref, flipped_ref)
    for x in range(PLANES):
        zero_rows(taps, lane(x * RPAD))
        zero_rows(cots, lane(x * RPAD))
    for x in range(PLANES):
        fetches[2 * x].wait()
        fetches[2 * x + 1].wait()
        rows = turned(act_ref[x], store.at[2 * x])
        fill_taps(taps, plane_at(x), rows)
        cot_rows = turned(cot_ref[x], store.at[2 * x + 1])
        fill_rows(cots, plane_at(x), cot_rows)
        for y in range(ROWS):
            turned_act[x, y] = rows[y].astype(bf16)
            turned_cot[x, y] = cot_rows[y].astype(bf16)

    def put(slot, value):
        out_ref[slot] = value

    def blocks(value, count):
        return [value[i * TAPS : (i + 1) * TAPS] for i in range(count)]

    plane = odd_ref[0] * (PLANES - 1)
    one_ref[...] = cot_ref[plane]
    two_ref[...] = cot_ref[PLANES - 1 - plane]
    near = (-1, 0, 1)
    sums = {}

    def add(key, value):
        sums[key] = value if key not in sums else sums[key] + value

    for x in range(PLANES):
        stay = jnp.concatenate(
            [taps[:, pl.ds(plane_at(x), WIDTH)], cots[:, pl.ds(plane_at(x), WIDTH)]], 0
        )
        level = dot_nt(shifted(taps, x, (0, 1, 2)), stay)
        zero, one, two = blocks(level, 3)
        cot_rows = [dot_nt(shifted(cots, x, near), stay)]
        if x + 1 < PLANES:
            up = dot_nt(shifted(taps, x + 1, (0, 1, 2, -1, -2)), stay)
            add("x1", up)
            cot_rows.append(dot_nt(shifted(cots, x + 1, near), stay))
            add("w2", cot_rows[1])
        if x >= 1:
            add("w0", dot_nt(shifted(cots, x - 1, near), stay))
        add("w1", cot_rows[0])
        if x + 2 < PLANES:
            add("x2", dot_nt(shifted(taps, x + 2, (0, 1, 2, -1, -2)), stay))
        edge = {}
        for name, row in (("F", 0), ("L", ROWS - 1)):
            stay_row = taps[:, pl.ds(plane_at(x, row), LANES)]
            count = min(3, PLANES - x)
            moving = jnp.concatenate(
                [taps[:, pl.ds(plane_at(x + i, row), LANES)] for i in range(count)], 0
            )
            edge_sum = blocks(jnp.pad(dot_nt(moving, stay_row), ((0, 0), (0, C))), count)
            edge[name] = edge_sum[0]
            for i in range(1, count):
                add((name, i), edge_sum[i])
        for i, value in enumerate((zero, edge["F"], edge["L"], one, two)):
            add(("level", i), value)
            if x == 0:
                put(A_P0 + i, value)
            if x == PLANES - 1:
                put(A_P3 + i, value)
    for i in range(5):
        put(A_X0 + i, sums[("level", i)])
    for base, name, i in ((A_X1, "x1", 1), (A_X2, "x2", 2)):
        whole = blocks(sums[name], 5)
        for j, value in enumerate((whole[0], sums[("F", i)], sums[("L", i)], *whole[1:])):
            put(base + j, value)
    wg_ref[0] = sums["w2"]
    wg_ref[1] = sums["w1"]
    wg_ref[2] = sums["w0"]


def gram_outer(
    core_ref, first_ref, last_ref, odd_ref, in_ref, wg_ref, act_ref, one_ref, two_ref, cot_ref,
    keep_ref, send_ref, taps, cots, out_ref, store,
):
    below, above = halo_planes(odd_ref[0] == 1, one_ref, two_ref)
    for index in range(6):
        zero_rows(taps, lane(index * RPAD))
        if index in (0, 2, 3, 4, 5):
            if index == 0:
                rows = turned(below, store.at[0])
            elif index == 5:
                rows = turned(above, store.at[1])
            else:
                rows = rows_of(act_ref[index - 1])
            fill_taps(taps, plane_at(index), rows)
    for slot, x in ((0, 0), (1, 3)):
        zero_rows(cots, lane(slot * RPAD))
        fill_rows(cots, plane_at(slot), rows_of(cot_ref[x]))

    def stay(index):
        return taps[:, pl.ds(plane_at(index), WIDTH)]

    five = (0, 1, 2, -1, -2)
    near = (-1, 0, 1)
    own = core_ref[0]
    first = first_ref[0].astype(f32)
    last = last_ref[0].astype(f32)

    def blocks(value, count):
        return [value[i * TAPS : (i + 1) * TAPS] for i in range(count)]

    def padded(value):
        return jnp.concatenate([value, jnp.zeros((value.shape[0], LANES - TAPS), f32)], 1)

    low = stay(0)
    gap = jnp.zeros((LANES - TAPS, WIDTH), bf16)
    top = dot_nt(shifted(taps, 5, five), jnp.concatenate([stay(4), gap, stay(3), gap], 0))
    x1 = blocks(top[:, :LANES], 5)
    x2 = blocks(top[:, LANES:] + dot_nt(shifted(taps, 2, five), jnp.concatenate([low, gap], 0)), 5)
    w_low = dot_nt(shifted(cots, 0, near), low)
    w_high = dot_nt(shifted(cots, 1, near), stay(5))

    def edge(left, right, row):
        return padded(dot_nt(
            taps[:, pl.ds(plane_at(left, row), LANES)], taps[:, pl.ds(plane_at(right, row), LANES)]
        ))

    wide = jnp.zeros((TAPS, LANES - TAPS), f32)
    wsums = (
        wg_ref[0] + jnp.concatenate([w_low, wide], 1),
        wg_ref[1],
        wg_ref[2] + jnp.concatenate([w_high, wide], 1),
    )
    at = lax.broadcasted_iota(jnp.int32, (TAPS, LANES), 1)

    def piece(t):
        if t > GRAD:
            return jnp.zeros((C, LANES), f32)
        if t == GRAD:
            return wsums[1][C : 2 * C]
        a, b, c = t // 9, t // 3 % 3, t % 3
        return pltpu.roll(wsums[a][(2 - b) * C : (3 - b) * C], TAPS - c * C, 1)

    def put(slot, value):
        extra = piece(slot)
        high = extra.astype(bf16).astype(f32)
        extra = jnp.concatenate([high, extra - high, jnp.zeros((C, LANES), f32)], 0)
        out_ref[(slot // HALF) ^ own, slot % HALF] = jnp.where(at < TAPS, value, extra).astype(bf16)

    def cut(value):
        return value

    for base, dx, parts, pairs in (
        (A_X1, 1, x1, ((5, 4),)),
        (A_X2, 2, x2, ((5, 3), (2, 0))),
    ):
        whole = cut(in_ref[base]) + parts[0]
        put(SLOT[(dx, "0")], whole)
        for j, (name, row) in enumerate((("f", 0), ("l", ROWS - 1))):
            edge_sum = cut(in_ref[base + 1 + j])
            for left, right in pairs:
                edge_sum = edge_sum + edge(left, right, row)
            put(SLOT[(dx, name)], whole - edge_sum)
        for j, dy in enumerate((1, 2, -1, -2)):
            put(SLOT[(dx, dy)], cut(in_ref[base + 3 + j]) + parts[1 + j])
    for name in ("0", "f", "l"):
        values = [cut(in_ref[A_X0 + i]) for i in range(5)]
        if name == "f":
            values = [v - first * cut(in_ref[A_P0 + i]) for i, v in enumerate(values)]
        if name == "l":
            values = [v - last * cut(in_ref[A_P3 + i]) for i, v in enumerate(values)]
        put(SLOT[(name, "0")], values[0])
        put(SLOT[(name, "f")], values[0] - values[1])
        put(SLOT[(name, "l")], values[0] - values[2])
        put(SLOT[(name, 1)], values[3])
        put(SLOT[(name, 2)], values[4])
    for slot in range(len(CLASSES), BLOCKS):
        put(slot, jnp.zeros((TAPS, LANES), f32))
    keep_ref[...] = out_ref[0]
    send_ref[...] = out_ref[1]


def settle(value):
    at = lax.broadcasted_iota(jnp.int32, (C, LANES), 1)
    first, second = value[:C], value[C : 2 * C]
    both = first + second
    high = both.astype(bf16).astype(f32)
    first = jnp.where(at < TAPS, first, high)
    second = jnp.where(at < TAPS, second, both - high)
    return jnp.concatenate([first, second, value[2 * C :]], 0).astype(bf16)


def settle_all(value):
    row = lax.broadcasted_iota(jnp.int32, value.shape, value.ndim - 2)
    at = lax.broadcasted_iota(jnp.int32, value.shape, value.ndim - 1)
    swapped = jnp.concatenate(
        [value[..., C : 2 * C, :], value[..., :C, :], value[..., 2 * C :, :]], -2
    )
    both = value + swapped
    high = lax.reduce_precision(both, 8, 7)
    piece = jnp.where(row < C, high, both - high)
    return jnp.where((at < TAPS) | (row >= 2 * C), value, piece).astype(bf16)


def add_kernel(keep_ref, arrived_ref, out_ref):
    for i in range(HALF):
        out_ref[i] = settle(keep_ref[i].astype(f32) + arrived_ref[i].astype(f32))


def sum_kernel(parts_ref, out_ref):
    total = parts_ref[0].astype(f32)
    for i in range(1, parts_ref.shape[0]):
        total = total + parts_ref[i].astype(f32)
    total = settle(total)
    for i in range(out_ref.shape[0]):
        out_ref[i] = total


def conv_kernel(
    odd_ref, act_ref, cot_ref, act_one, act_two, cot_one, cot_two, w_ref, flipped_ref,
    out_ref, back_ref,
    act_taps, cot_taps, store, halos,
):
    step = 2

    def fill(which, index):
        planes, dst = ((act_ref, act_taps), (cot_ref, cot_taps))[which]
        zero_rows(dst, lane(index * RPAD))
        if index in (0, PLANES + 1):
            pair = ((act_one, act_two), (cot_one, cot_two))[which]
            side = index // (PLANES + 1)
            rows = turned(halo_planes(odd_ref[0] == 1, *pair)[side], halos.at[which, side])
        else:
            rows = rows_of(planes[index - 1])
        fill_taps(dst, plane_at(index), rows)

    def products(which, x, weight):
        src = (act_taps, cot_taps)[which]
        plane = store.at[which, x]
        for y in range(0, ROWS, step):
            patch = jnp.concatenate(
                [
                    src[:, pl.ds(plane_at(x + 1 + dx, y + dy), step * LANES)]
                    for dx in (-1, 0, 1)
                    for dy in (-1, 0, 1)
                ],
                0,
            )
            value = jnp.dot(weight, patch, preferred_element_type=f32)
            for i in range(step):
                plane[(y + i) * C : (y + i + 1) * C, :] = value[:, lane(i) : lane(i + 1)]

    def put(which, x):
        target = (out_ref, back_ref)[which]
        for channel in range(C):
            target[channel, x] = store[which, x, pl.ds(channel, ROWS, stride=C), :].astype(bf16)

    weights = (w_ref[...], flipped_ref[...])
    fills = [(which, index) for which in (0, 1) for index in range(PLANES + 2)]
    for _ in range(3):
        fill(*fills.pop(0))
    before = None
    for which in (0, 1):
        for x in range(PLANES):
            products(which, x, weights[which])
            for _ in range(2 if which == 0 and x < 3 else 1):
                if fills:
                    fill(*fills.pop(0))
            if before:
                put(*before)
            before = (which, x)
    put(*before)


def split(value):
    high = value.astype(bf16)
    return high, (value - high.astype(f32)).astype(bf16)


def class_of(offset):
    return {0: "0", 1: "f", -1: "l"}[offset]


def finish_kernel(core_ref, mine_ref, other_ref, out_ref, factor):
    own = core_ref[0]

    def chosen(slot, rows=slice(None)):
        here = own == slot // HALF
        return jnp.where(here, mine_ref[slot % HALF, rows, :], other_ref[slot % HALF, rows, :])

    at = lax.broadcasted_iota(jnp.int32, (TAPS, LANES), 1)
    offsets = [(a, b) for a in (-1, 0, 1) for b in (-1, 0, 1)]
    tail = jnp.zeros((LANES - TAPS, LANES), f32)
    diag_row = lax.broadcasted_iota(jnp.int32, (LANES, LANES), 0)
    diag_col = lax.broadcasted_iota(jnp.int32, (LANES, LANES), 1)
    cache = {}

    def size(value):
        return jnp.sum(jnp.abs(value), axis=0, keepdims=True)

    def padded(slot, symmetric):
        if slot not in cache:
            value = jnp.where(at < TAPS, chosen(slot).astype(f32), 0.0)
            full = jnp.concatenate([value, tail], 0)
            turned = full if symmetric else full.T
            cache[slot] = (full.astype(bf16), turned.astype(bf16), size(full), size(turned), full)
        return cache[slot]

    sums = [jnp.zeros((1, LANES), f32) for _ in offsets]
    diagonal = jnp.zeros((LANES, LANES), f32)
    for i, (ax, ay) in enumerate(offsets):
        for j, (bx, by) in enumerate(offsets):
            dx, dy = bx - ax, by - ay
            if dx < 0 or (dx == 0 and dy < 0):
                continue
            key = (class_of(ax) if dx == 0 else dx, class_of(ay) if dy == 0 else dy)
            full, turned, size_full, size_turned, wide = padded(SLOT[key], i == j)
            factor[lane(j) : lane(j + 1), lane(i) : lane(i + 1)] = full
            sums[i] = sums[i] + size_full
            if i != j:
                factor[lane(i) : lane(i + 1), lane(j) : lane(j + 1)] = turned
                sums[j] = sums[j] + size_turned
            else:
                diagonal = diagonal + jnp.where(diag_row == diag_col, wide, 0.0)

    def extra(t):
        return chosen(t, slice(0, C)).astype(f32) + chosen(t, slice(C, 2 * C)).astype(f32)

    pieces = []
    for i in range(9):
        rows = jnp.zeros((C, LANES), f32)
        for c in range(3):
            moved = pltpu.roll(extra(3 * i + c), C + c * C, 1)
            rows = jnp.where(at[:C] // C == c, moved, rows)
        pieces.append(rows)
    wgrad = jnp.concatenate(pieces, 1) * (1.0 / CELLS)

    def exact(left, right):
        return jnp.dot(left, right, precision=lax.Precision.HIGHEST, preferred_element_type=f32)

    grad = extra(GRAD)[:, TAPS:LANES]
    row_id = lax.broadcasted_iota(jnp.int32, (C, C), 0)
    col_id = lax.broadcasted_iota(jnp.int32, (C, C), 1)
    eye = jnp.where(row_id == col_id, 1.0, 0.0).astype(f32)
    scaled = grad * (C / jnp.sum(grad * eye)) + DAMPING * eye
    inverse = eye / jnp.max(jnp.sum(jnp.abs(scaled), axis=1))

    scale = ORDER / jnp.sum(diagonal)
    bound = scale * jnp.max(jnp.concatenate(sums, 0)) + DAMPING
    step = scale / bound
    keep = 1.0 - DAMPING / bound
    value = wgrad
    half = None
    for sweep in range(2**ITERS - 1):
        high, low = split(value)
        product = jnp.dot(jnp.concatenate([high, low], 0), factor[...], preferred_element_type=f32)
        if sweep < 2 * ITERS:
            if sweep % 2 == 0:
                half = exact(inverse, scaled)
            else:
                inverse = 2.0 * inverse - exact(half, inverse)
        value = wgrad + keep * value - step * (product[:C] + product[C:])
    right = value * (1.0 / bound)
    applied = exact(inverse, right)
    quadratic = jnp.sum(applied * wgrad)
    result = applied * jnp.sqrt(C * ORDER / quadratic)
    out_ref[...] = jnp.concatenate([result[:, lane(i) : lane(i) + TAPS] for i in range(9)], 1)


SMEM = pl.BlockSpec(memory_space=pltpu.SMEM)
WHOLE = pl.BlockSpec(memory_space=pltpu.VMEM)
IN_HBM = pl.BlockSpec(memory_space=pltpu.HBM)


def call(kernel, shapes, scratch, inputs, scalars=0, flops=0, mib=16, specs=None, out_specs=None):
    return pl.pallas_call(
        kernel,
        out_shape=shapes,
        in_specs=specs or [SMEM] * scalars + [WHOLE] * (len(inputs) - scalars),
        out_specs=out_specs or jax.tree.map(lambda _: WHOLE, shapes),
        scratch_shapes=scratch,
        compiler_params=pltpu.CompilerParams(vmem_limit_bytes=mib * MIB),
        cost_estimate=pl.CostEstimate(flops=flops, bytes_accessed=1 << 20, transcendentals=0),
    )(*inputs)


def edge_kernel(odd_ref, act, one_ref, two_ref, sems):
    plane = odd_ref[0] * (PLANES - 1)
    copies = [
        pltpu.make_async_copy(act.at[:, plane], one_ref, sems.at[0]),
        pltpu.make_async_copy(act.at[:, PLANES - 1 - plane], two_ref, sems.at[1]),
    ]
    for copy in copies:
        copy.start()
    for copy in copies:
        copy.wait()


def edge_planes(odd, act):
    plane = pltpu.VMEM((C, ROWS, LANES), bf16)
    return call(
        edge_kernel,
        (plane, plane),
        [pltpu.SemaphoreType.DMA((2,))],
        (odd, act),
        mib=4,
        specs=[SMEM, IN_HBM],
    )


def conv(odd, act, cot, halos, weight, flipped):
    taps = pltpu.VMEM((TAPS, 6 * RPAD * LANES), bf16)
    shape = jax.ShapeDtypeStruct((C, PLANES, ROWS, LANES), bf16)
    return call(
        conv_kernel,
        (shape, shape),
        [
            taps,
            taps,
            pltpu.VMEM((2, PLANES, C * ROWS, LANES), f32),
            pltpu.VMEM((2, 2, C * ROWS, LANES), f32),
        ],
        (odd, act, cot, *halos, weight, flipped),
        scalars=1,
        flops=20 * 10**9,
        mib=20,
    )


def body(activations, cotangent, weight):
    space = ("y", "x", "z_lo")
    size = lax.axis_size(space)
    rounds = [
        [pair for i in range(start, size - 1, 2) for pair in ((i, i + 1), (i + 1, i))]
        for start in (1, 0)
    ]
    hold = lax.optimization_barrier

    where = lax.axis_index(space)
    core = lax.axis_index("core").astype(jnp.int32).reshape(1)
    first = (where == 0).astype(jnp.int32).reshape(1)
    last = (where == size - 1).astype(jnp.int32).reshape(1)
    odd = (where % 2).astype(jnp.int32).reshape(1)
    activations, cotangent, core, first, last, odd = hold(
        (activations, cotangent, core, first, last, odd)
    )
    act = pltpu.with_memory_space_constraint(activations[0], pltpu.HBM)
    cot = pltpu.with_memory_space_constraint(cotangent[0], pltpu.HBM)
    act_one, act_two = edge_planes(odd, act)
    act_one = lax.ppermute(act_one, space, rounds[0])
    act_two = lax.ppermute(act_two, space, rounds[1])
    turned_shape = pltpu.VMEM((PLANES, ROWS, C, LANES), bf16)
    sums, wsums, turned_act, turned_cot, flipped, cot_one, cot_two = call(
        gram_inner,
        (
            pltpu.VMEM((A_BLOCKS, TAPS, LANES), f32),
            pltpu.VMEM((3, TAPS, LANES), f32),
            turned_shape,
            turned_shape,
            jax.ShapeDtypeStruct((C, ORDER), bf16),
            jax.ShapeDtypeStruct((C, ROWS, LANES), bf16),
            jax.ShapeDtypeStruct((C, ROWS, LANES), bf16),
        ),
        [
            pltpu.VMEM((TAPS, PLANES * RPAD * LANES), bf16),
            pltpu.VMEM((C, PLANES * RPAD * LANES), bf16),
            pltpu.VMEM((2 * PLANES, C * ROWS, LANES), f32),
            pltpu.VMEM((PLANES, C, ROWS, LANES), bf16),
            pltpu.VMEM((PLANES, C, ROWS, LANES), bf16),
            pltpu.SemaphoreType.DMA((2 * PLANES,)),
        ],
        (odd, act, cot, weight),
        specs=[SMEM, IN_HBM, IN_HBM, WHOLE],
        flops=24 * 10**9 // 4,
        mib=MIB_INNER,
    )
    cot_one = lax.ppermute(cot_one, space, rounds[0])
    cot_two = lax.ppermute(cot_two, space, rounds[1])
    blocks_half = jax.ShapeDtypeStruct((HALF, TAPS, LANES), bf16)
    keep, send = call(
        gram_outer,
        (blocks_half, blocks_half),
        [
            pltpu.VMEM((TAPS, 6 * RPAD * LANES), bf16),
            pltpu.VMEM((C, 2 * RPAD * LANES), bf16),
            pltpu.VMEM((2, HALF, TAPS, LANES), bf16),
            pltpu.VMEM((2, C * ROWS, LANES), f32),
        ],
        (core, first, last, odd, sums, wsums, turned_act, act_one, act_two, turned_cot),
        scalars=4,
        flops=10**9,
        mib=MIB_OUTER,
    )

    swap = [(0, 1), (1, 0)]
    arrived = lax.ppermute(send, "core", swap)
    mine = call(add_kernel, blocks_half, [], (keep, arrived), mib=4)
    parts = lax.all_to_all(mine, ("y", "x"), 0, 0, tiled=True)
    depth = lax.axis_size(("z_hi", "z_lo"))
    block = call(sum_kernel, jax.ShapeDtypeStruct((depth, TAPS, LANES), bf16), [], (parts,), mib=4)
    block, act, cot = hold((block, turned_act, turned_cot))
    parts = lax.all_to_all(block, ("z_hi", "z_lo"), 0, 0, tiled=True)
    halos = (act_one, act_two, cot_one, cot_two)
    out, back = conv(odd, act, cot, halos, weight, flipped)
    parts, out, back = hold((parts, out, back))
    block = settle_all(jnp.sum(parts.astype(f32), axis=0))
    block = jnp.broadcast_to(block, (HALF, TAPS, LANES))
    whole = lax.all_to_all(block, ("y", "x"), 0, 0, tiled=True)
    other = lax.ppermute(whole, "core", swap)
    precond = call(
        finish_kernel,
        jax.ShapeDtypeStruct((C, ORDER), f32),
        [pltpu.VMEM((WIDE, WIDE), bf16)],
        (core, whole, other),
        scalars=1,
        flops=10**9,
    )
    return out[None], back[None], precond


def solution(mesh):
    fine = Mesh(mesh.devices.reshape(2, 2, 4, 4, 4), ("z_hi", "core", "y", "x", "z_lo"))
    spec = P(("z_hi", "core"), None, ("y", "x", "z_lo"), None, None)
    return jax.shard_map(
        body,
        mesh=fine,
        in_specs=(spec, spec, P()),
        out_specs=(spec, spec, P()),
        check_vma=False,
    )
```

```python
import functools

import jax
import jax.numpy as jnp
from jax import lax
from jax.experimental import pallas as pl
from jax.experimental.pallas import tpu as pltpu
from jax.sharding import Mesh
from jax.sharding import PartitionSpec as P

ITERS = 3
DAMPING = 0.1
C = 32
PLANES = 4
ROWS = 16
LANES = 128
RPAD = ROWS + 4
TAPS = 3 * C
ORDER = 27 * C
WIDE = 9 * LANES
CELLS = 2097152
MIB = 1024 * 1024
MIB_INNER, MIB_OUTER = 16, 16
NT = (((1,), (1,)), ((), ()))
f32 = jnp.float32
bf16 = jnp.bfloat16


CLASSES = []
for _x in ("0", "f", "l"):
    for _y in ("0", "f", "l", 1, 2):
        CLASSES.append((_x, _y))
for _x in (1, 2):
    for _y in ("0", "f", "l", 1, 2, -1, -2):
        CLASSES.append((_x, _y))
SLOT = {key: index for index, key in enumerate(CLASSES)}
GRAD = 27
BLOCKS = 32
HALF = BLOCKS // 2


def lane(row):
    return row * LANES


def turned(plane, store):
    store[...] = plane.astype(f32).reshape(C * ROWS, LANES)
    return [store[pl.ds(y, C, stride=ROWS), :] for y in range(ROWS)]


def halo_planes(odd, one_ref, two_ref):
    one, two = one_ref[...].astype(f32), two_ref[...].astype(f32)
    return jnp.where(odd, two, one), jnp.where(odd, one, two)


def rows_of(plane):
    return [plane[y].astype(f32) for y in range(ROWS)]


def fill_taps(dst, col, rows):
    at = lax.broadcasted_iota(jnp.int32, (C, LANES), 1)
    for y in range(ROWS):
        here = pl.ds(col + lane(y), LANES)
        before = jnp.where(at == 0, 0.0, pltpu.roll(rows[y], 1, 1))
        after = jnp.where(at == LANES - 1, 0.0, pltpu.roll(rows[y], LANES - 1, 1))
        dst[0:C, here] = before.astype(bf16)
        dst[C : 2 * C, here] = rows[y].astype(bf16)
        dst[2 * C : 3 * C, here] = after.astype(bf16)


def fill_rows(dst, col, rows):
    for y in range(ROWS):
        dst[:, pl.ds(col + lane(y), LANES)] = rows[y].astype(bf16)


def zero_rows(dst, col):
    zero = jnp.zeros((dst.shape[0], 2 * LANES), dst.dtype)
    dst[:, pl.ds(col, 2 * LANES)] = zero
    dst[:, pl.ds(col + lane(ROWS + 2), 2 * LANES)] = zero


def plane_at(index, row=0):
    return lane(index * RPAD + 2 + row)


def dot_nt(left, right):
    return lax.dot_general(left, right, NT, preferred_element_type=f32)


WIDTH = ROWS * LANES


def shifted(ref, index, rows, width=WIDTH):
    return jnp.concatenate([ref[:, pl.ds(plane_at(index, dy), width)] for dy in rows], 0)


A_P0, A_P3, A_X0 = 0, 5, 10
A_X1, A_X2 = 15, 22
A_BLOCKS = 29


def flip_taps(w_ref, flipped_ref):
    wide = jnp.concatenate([w_ref[...].astype(f32), jnp.zeros((C, 7 * LANES - ORDER), f32)], 1)
    tall = jnp.concatenate([wide, jnp.zeros((LANES - C, 7 * LANES), f32)], 0).T
    for group in range(7):
        total = jnp.zeros((C, LANES), f32)
        for place in range(4):
            tap = 26 - 4 * group - place
            if tap >= 0:
                block = tall[tap * C : (tap + 1) * C, :]
                total = total + (pltpu.roll(block, place * C, 1) if place else block)
        width = min(LANES, ORDER - lane(group))
        flipped_ref[:, lane(group) : lane(group) + width] = total[:, :width].astype(bf16)


def gram_inner(
    odd_ref, act_hbm, cot_hbm,
    out_ref, wg_ref, turned_act, turned_cot, one_ref, two_ref,
    taps, cots, store, act_ref, cot_ref, sems,
):
    fetches = []
    for x in range(PLANES):
        for i, (source, target) in enumerate(((act_hbm, act_ref), (cot_hbm, cot_ref))):
            fetches.append(
                pltpu.make_async_copy(source.at[:, x], target.at[x], sems.at[2 * x + i])
            )
    for fetch in fetches:
        fetch.start()
    for x in range(PLANES):
        zero_rows(taps, lane(x * RPAD))
        zero_rows(cots, lane(x * RPAD))
    for x in range(PLANES):
        fetches[2 * x].wait()
        fetches[2 * x + 1].wait()
        rows = turned(act_ref[x], store.at[2 * x])
        fill_taps(taps, plane_at(x), rows)
        cot_rows = turned(cot_ref[x], store.at[2 * x + 1])
        fill_rows(cots, plane_at(x), cot_rows)
        for y in range(ROWS):
            turned_act[x, y] = rows[y].astype(bf16)
            turned_cot[x, y] = cot_rows[y].astype(bf16)

    def put(slot, value):
        out_ref[slot] = value

    def blocks(value, count):
        return [value[i * TAPS : (i + 1) * TAPS] for i in range(count)]

    plane = odd_ref[0] * (PLANES - 1)
    one_ref[...] = cot_ref[plane]
    two_ref[...] = cot_ref[PLANES - 1 - plane]
    near = (-1, 0, 1)
    sums = {}

    def add(key, value):
        sums[key] = value if key not in sums else sums[key] + value

    stays = [
        jnp.concatenate(
            [taps[:, pl.ds(plane_at(x), WIDTH)], cots[:, pl.ds(plane_at(x), WIDTH)]], 0
        )
        for x in range(PLANES)
    ]
    for x in range(PLANES):
        stay = stays[x]
        level = dot_nt(shifted(taps, x, (0, 1, 2)), stay)
        zero, one, two = blocks(level, 3)
        cot_rows = [dot_nt(shifted(cots, x, near), stay)]
        if x + 1 < PLANES:
            moving = shifted(taps, x + 1, (0, 1, 2, -1, -2))
            if x == 0:
                add("x1", dot_nt(moving, stay))
            else:
                pair = dot_nt(moving, jnp.concatenate([stay, stays[x - 1]], 0))
                add("x1", pair[:, :LANES])
                add("x2", pair[:, LANES:])
            cot_rows.append(dot_nt(shifted(cots, x + 1, near), stay))
            add("w2", cot_rows[1])
        if x >= 1:
            add("w0", dot_nt(shifted(cots, x - 1, near), stay))
        add("w1", cot_rows[0])
        edge = {}
        for name, row in (("F", 0), ("L", ROWS - 1)):
            stay_row = taps[:, pl.ds(plane_at(x, row), LANES)]
            count = min(3, PLANES - x)
            moving = jnp.concatenate(
                [taps[:, pl.ds(plane_at(x + i, row), LANES)] for i in range(count)], 0
            )
            edge_sum = blocks(jnp.pad(dot_nt(moving, stay_row), ((0, 0), (0, C))), count)
            edge[name] = edge_sum[0]
            for i in range(1, count):
                add((name, i), edge_sum[i])
        for i, value in enumerate((zero, edge["F"], edge["L"], one, two)):
            add(("level", i), value)
            if x == 0:
                put(A_P0 + i, value)
            if x == PLANES - 1:
                put(A_P3 + i, value)
    for i in range(5):
        put(A_X0 + i, sums[("level", i)])
    for base, name, i in ((A_X1, "x1", 1), (A_X2, "x2", 2)):
        whole = blocks(sums[name], 5)
        for j, value in enumerate((whole[0], sums[("F", i)], sums[("L", i)], *whole[1:])):
            put(base + j, value)
    wg_ref[0] = sums["w2"]
    wg_ref[1] = sums["w1"]
    wg_ref[2] = sums["w0"]


def gram_outer(
    core_ref, first_ref, last_ref, odd_ref, in_ref, wg_ref, act_ref, one_ref, two_ref, cot_ref,
    keep_ref, send_ref, taps, cots, out_ref, store,
):
    below, above = halo_planes(odd_ref[0] == 1, one_ref, two_ref)
    for index in range(6):
        zero_rows(taps, lane(index * RPAD))
        if index in (0, 2, 3, 4, 5):
            if index == 0:
                rows = turned(below, store.at[0])
            elif index == 5:
                rows = turned(above, store.at[1])
            else:
                rows = rows_of(act_ref[index - 1])
            fill_taps(taps, plane_at(index), rows)
    for slot, x in ((0, 0), (1, 3)):
        zero_rows(cots, lane(slot * RPAD))
        fill_rows(cots, plane_at(slot), rows_of(cot_ref[x]))

    def stay(index):
        return taps[:, pl.ds(plane_at(index), WIDTH)]

    five = (0, 1, 2, -1, -2)
    near = (-1, 0, 1)
    own = core_ref[0]
    first = first_ref[0].astype(f32)
    last = last_ref[0].astype(f32)

    def blocks(value, count):
        return [value[i * TAPS : (i + 1) * TAPS] for i in range(count)]

    def padded(value):
        return jnp.concatenate([value, jnp.zeros((value.shape[0], LANES - TAPS), f32)], 1)

    low = stay(0)
    gap = jnp.zeros((LANES - TAPS, WIDTH), bf16)
    top = dot_nt(shifted(taps, 5, five), jnp.concatenate([stay(4), gap, stay(3), gap], 0))
    x1 = blocks(top[:, :LANES], 5)
    x2 = blocks(top[:, LANES:] + dot_nt(shifted(taps, 2, five), jnp.concatenate([low, gap], 0)), 5)
    w_low = dot_nt(shifted(cots, 0, near), low)
    w_high = dot_nt(shifted(cots, 1, near), stay(5))

    def edge(left, right, row):
        return padded(dot_nt(
            taps[:, pl.ds(plane_at(left, row), LANES)], taps[:, pl.ds(plane_at(right, row), LANES)]
        ))

    wide = jnp.zeros((TAPS, LANES - TAPS), f32)
    wsums = (
        wg_ref[0] + jnp.concatenate([w_low, wide], 1),
        wg_ref[1],
        wg_ref[2] + jnp.concatenate([w_high, wide], 1),
    )
    at = lax.broadcasted_iota(jnp.int32, (TAPS, LANES), 1)

    def piece(t):
        if t > GRAD:
            return jnp.zeros((C, LANES), f32)
        if t == GRAD:
            return wsums[1][C : 2 * C]
        a, b, c = t // 9, t // 3 % 3, t % 3
        return pltpu.roll(wsums[a][(2 - b) * C : (3 - b) * C], TAPS - c * C, 1)

    def put(slot, value):
        extra = piece(slot)
        high = extra.astype(bf16).astype(f32)
        extra = jnp.concatenate([high, extra - high, jnp.zeros((C, LANES), f32)], 0)
        out_ref[(slot // HALF) ^ own, slot % HALF] = jnp.where(at < TAPS, value, extra).astype(bf16)

    def cut(value):
        return value

    for base, dx, parts, pairs in (
        (A_X1, 1, x1, ((5, 4),)),
        (A_X2, 2, x2, ((5, 3), (2, 0))),
    ):
        whole = cut(in_ref[base]) + parts[0]
        put(SLOT[(dx, "0")], whole)
        for j, (name, row) in enumerate((("f", 0), ("l", ROWS - 1))):
            edge_sum = cut(in_ref[base + 1 + j])
            for left, right in pairs:
                edge_sum = edge_sum + edge(left, right, row)
            put(SLOT[(dx, name)], whole - edge_sum)
        for j, dy in enumerate((1, 2, -1, -2)):
            put(SLOT[(dx, dy)], cut(in_ref[base + 3 + j]) + parts[1 + j])
    for name in ("0", "f", "l"):
        values = [cut(in_ref[A_X0 + i]) for i in range(5)]
        if name == "f":
            values = [v - first * cut(in_ref[A_P0 + i]) for i, v in enumerate(values)]
        if name == "l":
            values = [v - last * cut(in_ref[A_P3 + i]) for i, v in enumerate(values)]
        put(SLOT[(name, "0")], values[0])
        put(SLOT[(name, "f")], values[0] - values[1])
        put(SLOT[(name, "l")], values[0] - values[2])
        put(SLOT[(name, 1)], values[3])
        put(SLOT[(name, 2)], values[4])
    for slot in range(len(CLASSES), BLOCKS):
        put(slot, jnp.zeros((TAPS, LANES), f32))
    keep_ref[...] = out_ref[0]
    send_ref[...] = out_ref[1]


def settle(value):
    at = lax.broadcasted_iota(jnp.int32, (C, LANES), 1)
    first, second = value[:C], value[C : 2 * C]
    both = first + second
    high = both.astype(bf16).astype(f32)
    first = jnp.where(at < TAPS, first, high)
    second = jnp.where(at < TAPS, second, both - high)
    return jnp.concatenate([first, second, value[2 * C :]], 0).astype(bf16)


def settle_all(value):
    row = lax.broadcasted_iota(jnp.int32, value.shape, value.ndim - 2)
    at = lax.broadcasted_iota(jnp.int32, value.shape, value.ndim - 1)
    swapped = jnp.concatenate(
        [value[..., C : 2 * C, :], value[..., :C, :], value[..., 2 * C :, :]], -2
    )
    both = value + swapped
    high = lax.reduce_precision(both, 8, 7)
    piece = jnp.where(row < C, high, both - high)
    return jnp.where((at < TAPS) | (row >= 2 * C), value, piece).astype(bf16)


def add_kernel(keep_ref, arrived_ref, out_ref):
    for i in range(HALF):
        out_ref[i] = settle(keep_ref[i].astype(f32) + arrived_ref[i].astype(f32))


def sum_kernel(parts_ref, out_ref):
    total = parts_ref[0].astype(f32)
    for i in range(1, parts_ref.shape[0]):
        total = total + parts_ref[i].astype(f32)
    total = settle(total)
    for i in range(out_ref.shape[0]):
        out_ref[i] = total


def conv_kernel(
    odd_ref, act_ref, cot_ref, act_one, act_two, cot_one, cot_two, w_ref,
    out_ref, back_ref,
    act_taps, cot_taps, store, halos, flipped_ref,
):
    step = 2

    def fill(which, index):
        planes, dst = ((act_ref, act_taps), (cot_ref, cot_taps))[which]
        zero_rows(dst, lane(index * RPAD))
        if index in (0, PLANES + 1):
            pair = ((act_one, act_two), (cot_one, cot_two))[which]
            side = index // (PLANES + 1)
            rows = turned(halo_planes(odd_ref[0] == 1, *pair)[side], halos.at[which, side])
        else:
            rows = rows_of(planes[index - 1])
        fill_taps(dst, plane_at(index), rows)

    def products(which, x, weight):
        src = (act_taps, cot_taps)[which]
        plane = store.at[which, x]
        for y in range(0, ROWS, step):
            patch = jnp.concatenate(
                [
                    src[:, pl.ds(plane_at(x + 1 + dx, y + dy), step * LANES)]
                    for dx in (-1, 0, 1)
                    for dy in (-1, 0, 1)
                ],
                0,
            )
            value = jnp.dot(weight, patch, preferred_element_type=f32)
            for i in range(step):
                plane[(y + i) * C : (y + i + 1) * C, :] = value[:, lane(i) : lane(i + 1)]

    def put(which, x):
        target = (out_ref, back_ref)[which]
        for channel in range(C):
            target[channel, x] = store[which, x, pl.ds(channel, ROWS, stride=C), :].astype(bf16)

    flip_taps(w_ref, flipped_ref)
    weights = (w_ref[...], flipped_ref[...])
    fills = [(which, index) for which in (0, 1) for index in range(PLANES + 2)]
    for _ in range(3):
        fill(*fills.pop(0))
    before = None
    for which in (0, 1):
        for x in range(PLANES):
            products(which, x, weights[which])
            for _ in range(2 if which == 0 and x < 3 else 1):
                if fills:
                    fill(*fills.pop(0))
            if before:
                put(*before)
            before = (which, x)
    put(*before)


def split(value):
    high = value.astype(bf16)
    return high, (value - high.astype(f32)).astype(bf16)


def class_of(offset):
    return {0: "0", 1: "f", -1: "l"}[offset]


def finish_kernel(core_ref, mine_ref, other_ref, out_ref, factor):
    own = core_ref[0]

    def chosen(slot, rows=slice(None)):
        here = own == slot // HALF
        return jnp.where(here, mine_ref[slot % HALF, rows, :], other_ref[slot % HALF, rows, :])

    at = lax.broadcasted_iota(jnp.int32, (TAPS, LANES), 1)
    offsets = [(a, b) for a in (-1, 0, 1) for b in (-1, 0, 1)]
    tail = jnp.zeros((LANES - TAPS, LANES), f32)
    diag_row = lax.broadcasted_iota(jnp.int32, (LANES, LANES), 0)
    diag_col = lax.broadcasted_iota(jnp.int32, (LANES, LANES), 1)
    cache = {}

    def size(value):
        return jnp.sum(jnp.abs(value), axis=0, keepdims=True)

    def padded(slot, symmetric):
        if slot not in cache:
            value = jnp.where(at < TAPS, chosen(slot).astype(f32), 0.0)
            full = jnp.concatenate([value, tail], 0)
            turned = full if symmetric else full.T
            cache[slot] = (full.astype(bf16), turned.astype(bf16), size(full), size(turned), full)
        return cache[slot]

    sums = [jnp.zeros((1, LANES), f32) for _ in offsets]
    diagonal = jnp.zeros((LANES, LANES), f32)
    for i, (ax, ay) in enumerate(offsets):
        for j, (bx, by) in enumerate(offsets):
            dx, dy = bx - ax, by - ay
            if dx < 0 or (dx == 0 and dy < 0):
                continue
            key = (class_of(ax) if dx == 0 else dx, class_of(ay) if dy == 0 else dy)
            full, turned, size_full, size_turned, wide = padded(SLOT[key], i == j)
            factor[lane(j) : lane(j + 1), lane(i) : lane(i + 1)] = full
            sums[i] = sums[i] + size_full
            if i != j:
                factor[lane(i) : lane(i + 1), lane(j) : lane(j + 1)] = turned
                sums[j] = sums[j] + size_turned
            else:
                diagonal = diagonal + jnp.where(diag_row == diag_col, wide, 0.0)

    def extra(t):
        return chosen(t, slice(0, C)).astype(f32) + chosen(t, slice(C, 2 * C)).astype(f32)

    pieces = []
    for i in range(9):
        rows = jnp.zeros((C, LANES), f32)
        for c in range(3):
            moved = pltpu.roll(extra(3 * i + c), C + c * C, 1)
            rows = jnp.where(at[:C] // C == c, moved, rows)
        pieces.append(rows)
    wgrad = jnp.concatenate(pieces, 1) * (1.0 / CELLS)

    def exact(left, right):
        return jnp.dot(left, right, precision=lax.Precision.HIGHEST, preferred_element_type=f32)

    grad = extra(GRAD)[:, TAPS:LANES]
    row_id = lax.broadcasted_iota(jnp.int32, (C, C), 0)
    col_id = lax.broadcasted_iota(jnp.int32, (C, C), 1)
    eye = jnp.where(row_id == col_id, 1.0, 0.0).astype(f32)
    scaled = grad * (C / jnp.sum(grad * eye)) + DAMPING * eye
    inverse = eye / jnp.max(jnp.sum(jnp.abs(scaled), axis=1))

    scale = ORDER / jnp.sum(diagonal)
    bound = scale * jnp.max(jnp.concatenate(sums, 0)) + DAMPING
    step = scale / bound
    keep = 1.0 - DAMPING / bound
    value = wgrad
    half = None
    for sweep in range(2**ITERS - 1):
        high, low = split(value)
        product = jnp.dot(jnp.concatenate([high, low], 0), factor[...], preferred_element_type=f32)
        if sweep < 2 * ITERS:
            if sweep % 2 == 0:
                half = exact(inverse, scaled)
            else:
                inverse = 2.0 * inverse - exact(half, inverse)
        value = wgrad + keep * value - step * (product[:C] + product[C:])
    right = value * (1.0 / bound)
    applied = exact(inverse, right)
    quadratic = jnp.sum(applied * wgrad)
    result = applied * jnp.sqrt(C * ORDER / quadratic)
    out_ref[...] = jnp.concatenate([result[:, lane(i) : lane(i) + TAPS] for i in range(9)], 1)


SMEM = pl.BlockSpec(memory_space=pltpu.SMEM)
WHOLE = pl.BlockSpec(memory_space=pltpu.VMEM)
IN_HBM = pl.BlockSpec(memory_space=pltpu.HBM)


def call(kernel, shapes, scratch, inputs, scalars=0, flops=0, mib=16, specs=None, out_specs=None):
    return pl.pallas_call(
        kernel,
        out_shape=shapes,
        in_specs=specs or [SMEM] * scalars + [WHOLE] * (len(inputs) - scalars),
        out_specs=out_specs or jax.tree.map(lambda _: WHOLE, shapes),
        scratch_shapes=scratch,
        compiler_params=pltpu.CompilerParams(vmem_limit_bytes=mib * MIB),
        cost_estimate=pl.CostEstimate(flops=flops, bytes_accessed=1 << 20, transcendentals=0),
    )(*inputs)


def edge_kernel(odd_ref, act, one_ref, two_ref, sems):
    plane = odd_ref[0] * (PLANES - 1)
    copies = [
        pltpu.make_async_copy(act.at[:, plane], one_ref, sems.at[0]),
        pltpu.make_async_copy(act.at[:, PLANES - 1 - plane], two_ref, sems.at[1]),
    ]
    for copy in copies:
        copy.start()
    for copy in copies:
        copy.wait()


def edge_planes(odd, act):
    plane = pltpu.VMEM((C, ROWS, LANES), bf16)
    return call(
        edge_kernel,
        (plane, plane),
        [pltpu.SemaphoreType.DMA((2,))],
        (odd, act),
        mib=4,
        specs=[SMEM, IN_HBM],
    )


def conv(odd, act, cot, halos, weight):
    taps = pltpu.VMEM((TAPS, 6 * RPAD * LANES), bf16)
    shape = jax.ShapeDtypeStruct((C, PLANES, ROWS, LANES), bf16)
    return call(
        conv_kernel,
        (shape, shape),
        [
            taps,
            taps,
            pltpu.VMEM((2, PLANES, C * ROWS, LANES), f32),
            pltpu.VMEM((2, 2, C * ROWS, LANES), f32),
            pltpu.VMEM((C, ORDER), bf16),
        ],
        (odd, act, cot, *halos, weight),
        scalars=1,
        flops=20 * 10**9,
        mib=20,
    )


def body(activations, cotangent, weight):
    space = ("y", "x", "z_lo")
    size = lax.axis_size(space)
    rounds = [
        [pair for i in range(start, size - 1, 2) for pair in ((i, i + 1), (i + 1, i))]
        for start in (1, 0)
    ]
    hold = lax.optimization_barrier

    where = lax.axis_index(space)
    core = lax.axis_index("core").astype(jnp.int32).reshape(1)
    first = (where == 0).astype(jnp.int32).reshape(1)
    last = (where == size - 1).astype(jnp.int32).reshape(1)
    odd = (where % 2).astype(jnp.int32).reshape(1)
    activations, cotangent, core, first, last, odd = hold(
        (activations, cotangent, core, first, last, odd)
    )
    act = pltpu.with_memory_space_constraint(activations[0], pltpu.HBM)
    cot = pltpu.with_memory_space_constraint(cotangent[0], pltpu.HBM)
    act_one, act_two = edge_planes(odd, act)
    act_one = lax.ppermute(act_one, space, rounds[0])
    act_two = lax.ppermute(act_two, space, rounds[1])
    turned_shape = pltpu.VMEM((PLANES, ROWS, C, LANES), bf16)
    sums, wsums, turned_act, turned_cot, cot_one, cot_two = call(
        gram_inner,
        (
            pltpu.VMEM((A_BLOCKS, TAPS, LANES), f32),
            pltpu.VMEM((3, TAPS, LANES), f32),
            turned_shape,
            turned_shape,
            jax.ShapeDtypeStruct((C, ROWS, LANES), bf16),
            jax.ShapeDtypeStruct((C, ROWS, LANES), bf16),
        ),
        [
            pltpu.VMEM((TAPS, PLANES * RPAD * LANES), bf16),
            pltpu.VMEM((C, PLANES * RPAD * LANES), bf16),
            pltpu.VMEM((2 * PLANES, C * ROWS, LANES), f32),
            pltpu.VMEM((PLANES, C, ROWS, LANES), bf16),
            pltpu.VMEM((PLANES, C, ROWS, LANES), bf16),
            pltpu.SemaphoreType.DMA((2 * PLANES,)),
        ],
        (odd, act, cot),
        specs=[SMEM, IN_HBM, IN_HBM],
        flops=24 * 10**9 // 4,
        mib=MIB_INNER,
    )
    cot_one = lax.ppermute(cot_one, space, rounds[0])
    cot_two = lax.ppermute(cot_two, space, rounds[1])
    blocks_half = jax.ShapeDtypeStruct((HALF, TAPS, LANES), bf16)
    keep, send = call(
        gram_outer,
        (blocks_half, blocks_half),
        [
            pltpu.VMEM((TAPS, 6 * RPAD * LANES), bf16),
            pltpu.VMEM((C, 2 * RPAD * LANES), bf16),
            pltpu.VMEM((2, HALF, TAPS, LANES), bf16),
            pltpu.VMEM((2, C * ROWS, LANES), f32),
        ],
        (core, first, last, odd, sums, wsums, turned_act, act_one, act_two, turned_cot),
        scalars=4,
        flops=10**9,
        mib=MIB_OUTER,
    )

    swap = [(0, 1), (1, 0)]
    arrived = lax.ppermute(send, "core", swap)
    mine = call(add_kernel, blocks_half, [], (keep, arrived), mib=4)
    parts = lax.all_to_all(mine, ("y", "x"), 0, 0, tiled=True)
    depth = lax.axis_size(("z_hi", "z_lo"))
    block = call(sum_kernel, jax.ShapeDtypeStruct((depth, TAPS, LANES), bf16), [], (parts,), mib=4)
    block, act, cot = hold((block, turned_act, turned_cot))
    parts = lax.all_to_all(block, ("z_hi", "z_lo"), 0, 0, tiled=True)
    halos = (act_one, act_two, cot_one, cot_two)
    out, back = conv(odd, act, cot, halos, weight)
    parts, out, back = hold((parts, out, back))
    block = settle_all(jnp.sum(parts.astype(f32), axis=0))
    block = jnp.broadcast_to(block, (HALF, TAPS, LANES))
    whole = lax.all_to_all(block, ("y", "x"), 0, 0, tiled=True)
    other = lax.ppermute(whole, "core", swap)
    precond = call(
        finish_kernel,
        jax.ShapeDtypeStruct((C, ORDER), f32),
        [pltpu.VMEM((WIDE, WIDE), bf16)],
        (core, whole, other),
        scalars=1,
        flops=10**9,
    )
    return out[None], back[None], precond


def solution(mesh):
    fine = Mesh(mesh.devices.reshape(2, 2, 4, 4, 4), ("z_hi", "core", "y", "x", "z_lo"))
    spec = P(("z_hi", "core"), None, ("y", "x", "z_lo"), None, None)
    return jax.shard_map(
        body,
        mesh=fine,
        in_specs=(spec, spec, P()),
        out_specs=(spec, spec, P()),
        check_vma=False,
    )
```

```python
import functools

import jax
import jax.numpy as jnp
from jax import lax
from jax.experimental import pallas as pl
from jax.experimental.pallas import tpu as pltpu
from jax.sharding import Mesh
from jax.sharding import PartitionSpec as P

ITERS = 3
DAMPING = 0.1
C = 32
PLANES = 4
ROWS = 16
LANES = 128
RPAD = ROWS + 4
TAPS = 3 * C
ORDER = 27 * C
WIDE = 9 * LANES
CELLS = 2097152
MIB = 1024 * 1024
MIB_INNER, MIB_OUTER = 16, 16
NT = (((1,), (1,)), ((), ()))
f32 = jnp.float32
bf16 = jnp.bfloat16


CLASSES = []
for _x in ("0", "f", "l"):
    for _y in ("0", "f", "l", 1, 2):
        CLASSES.append((_x, _y))
for _x in (1, 2):
    for _y in ("0", "f", "l", 1, 2, -1, -2):
        CLASSES.append((_x, _y))
SLOT = {key: index for index, key in enumerate(CLASSES)}
GRAD = 27
BLOCKS = 32
HALF = BLOCKS // 2


def lane(row):
    return row * LANES


def turned(plane, store):
    store[...] = plane.astype(f32).reshape(C * ROWS, LANES)
    return [store[pl.ds(y, C, stride=ROWS), :] for y in range(ROWS)]


def halo_planes(odd, one_ref, two_ref):
    one, two = one_ref[...].astype(f32), two_ref[...].astype(f32)
    return jnp.where(odd, two, one), jnp.where(odd, one, two)


def rows_of(plane):
    return [plane[y].astype(f32) for y in range(ROWS)]


def fill_taps(dst, col, rows):
    at = lax.broadcasted_iota(jnp.int32, (C, LANES), 1)
    for y in range(ROWS):
        here = pl.ds(col + lane(y), LANES)
        before = jnp.where(at == 0, 0.0, pltpu.roll(rows[y], 1, 1))
        after = jnp.where(at == LANES - 1, 0.0, pltpu.roll(rows[y], LANES - 1, 1))
        dst[0:C, here] = before.astype(bf16)
        dst[C : 2 * C, here] = rows[y].astype(bf16)
        dst[2 * C : 3 * C, here] = after.astype(bf16)


def fill_rows(dst, col, rows):
    for y in range(ROWS):
        dst[:, pl.ds(col + lane(y), LANES)] = rows[y].astype(bf16)


def zero_rows(dst, col):
    zero = jnp.zeros((dst.shape[0], 2 * LANES), dst.dtype)
    dst[:, pl.ds(col, 2 * LANES)] = zero
    dst[:, pl.ds(col + lane(ROWS + 2), 2 * LANES)] = zero


def plane_at(index, row=0):
    return lane(index * RPAD + 2 + row)


def dot_nt(left, right):
    return lax.dot_general(left, right, NT, preferred_element_type=f32)


WIDTH = ROWS * LANES


def shifted(ref, index, rows, width=WIDTH):
    return jnp.concatenate([ref[:, pl.ds(plane_at(index, dy), width)] for dy in rows], 0)


A_P0, A_P3, A_X0 = 0, 5, 10
A_X1, A_X2 = 15, 22
A_BLOCKS = 29


def flip_taps(w_ref, flipped_ref):
    wide = jnp.concatenate([w_ref[...].astype(f32), jnp.zeros((C, 7 * LANES - ORDER), f32)], 1)
    tall = jnp.concatenate([wide, jnp.zeros((LANES - C, 7 * LANES), f32)], 0).T
    for group in range(7):
        total = jnp.zeros((C, LANES), f32)
        for place in range(4):
            tap = 26 - 4 * group - place
            if tap >= 0:
                block = tall[tap * C : (tap + 1) * C, :]
                total = total + (pltpu.roll(block, place * C, 1) if place else block)
        width = min(LANES, ORDER - lane(group))
        flipped_ref[:, lane(group) : lane(group) + width] = total[:, :width].astype(bf16)


def gram_inner(
    odd_ref, act_hbm, cot_hbm,
    out_ref, wg_ref, turned_act, turned_cot, one_ref, two_ref,
    taps, cots, store, act_ref, cot_ref, sems,
):
    fetches = []
    for x in range(PLANES):
        for i, (source, target) in enumerate(((act_hbm, act_ref), (cot_hbm, cot_ref))):
            fetches.append(
                pltpu.make_async_copy(source.at[:, x], target.at[x], sems.at[2 * x + i])
            )
    for fetch in fetches:
        fetch.start()
    for x in range(PLANES):
        zero_rows(taps, lane(x * RPAD))
        zero_rows(cots, lane(x * RPAD))
    for x in range(PLANES):
        fetches[2 * x].wait()
        fetches[2 * x + 1].wait()
        rows = turned(act_ref[x], store.at[2 * x])
        fill_taps(taps, plane_at(x), rows)
        cot_rows = turned(cot_ref[x], store.at[2 * x + 1])
        fill_rows(cots, plane_at(x), cot_rows)
        for y in range(ROWS):
            turned_act[x, y] = rows[y].astype(bf16)
            turned_cot[x, y] = cot_rows[y].astype(bf16)

    def put(slot, value):
        out_ref[slot] = value

    def blocks(value, count):
        return [value[i * TAPS : (i + 1) * TAPS] for i in range(count)]

    plane = odd_ref[0] * (PLANES - 1)
    one_ref[...] = cot_ref[plane]
    two_ref[...] = cot_ref[PLANES - 1 - plane]
    near = (-1, 0, 1)
    sums = {}

    def add(key, value):
        sums[key] = value if key not in sums else sums[key] + value

    stays = [
        jnp.concatenate(
            [taps[:, pl.ds(plane_at(x), WIDTH)], cots[:, pl.ds(plane_at(x), WIDTH)]], 0
        )
        for x in range(PLANES)
    ]
    for x in range(PLANES):
        stay = stays[x]
        level = dot_nt(shifted(taps, x, (0, 1, 2)), stay)
        zero, one, two = blocks(level, 3)
        cot_rows = [dot_nt(shifted(cots, x, near), stay)]
        if x + 1 < PLANES:
            moving = shifted(taps, x + 1, (0, 1, 2, -1, -2))
            if x == 0:
                add("x1", dot_nt(moving, stay))
            else:
                pair = dot_nt(moving, jnp.concatenate([stay, stays[x - 1]], 0))
                add("x1", pair[:, :LANES])
                add("x2", pair[:, LANES:])
            cot_rows.append(dot_nt(shifted(cots, x + 1, near), stay))
            add("w2", cot_rows[1])
        if x >= 1:
            add("w0", dot_nt(shifted(cots, x - 1, near), stay))
        add("w1", cot_rows[0])
        edge = {}
        for name, row in (("F", 0), ("L", ROWS - 1)):
            stay_row = taps[:, pl.ds(plane_at(x, row), LANES)]
            count = min(3, PLANES - x)
            moving = jnp.concatenate(
                [taps[:, pl.ds(plane_at(x + i, row), LANES)] for i in range(count)], 0
            )
            edge_sum = blocks(jnp.pad(dot_nt(moving, stay_row), ((0, 0), (0, C))), count)
            edge[name] = edge_sum[0]
            for i in range(1, count):
                add((name, i), edge_sum[i])
        for i, value in enumerate((zero, edge["F"], edge["L"], one, two)):
            add(("level", i), value)
            if x == 0:
                put(A_P0 + i, value)
            if x == PLANES - 1:
                put(A_P3 + i, value)
    for i in range(5):
        put(A_X0 + i, sums[("level", i)])
    for base, name, i in ((A_X1, "x1", 1), (A_X2, "x2", 2)):
        whole = blocks(sums[name], 5)
        for j, value in enumerate((whole[0], sums[("F", i)], sums[("L", i)], *whole[1:])):
            put(base + j, value)
    wg_ref[0] = sums["w2"]
    wg_ref[1] = sums["w1"]
    wg_ref[2] = sums["w0"]


def gram_outer(
    core_ref, first_ref, last_ref, odd_ref, in_ref, wg_ref, act_ref, one_ref, two_ref, cot_ref,
    keep_ref, send_ref, taps, cots, out_ref, store,
):
    below, above = halo_planes(odd_ref[0] == 1, one_ref, two_ref)
    for index in range(6):
        zero_rows(taps, lane(index * RPAD))
        if index in (0, 2, 3, 4, 5):
            if index == 0:
                rows = turned(below, store.at[0])
            elif index == 5:
                rows = turned(above, store.at[1])
            else:
                rows = rows_of(act_ref[index - 1])
            fill_taps(taps, plane_at(index), rows)
    for slot, x in ((0, 0), (1, 3)):
        zero_rows(cots, lane(slot * RPAD))
        fill_rows(cots, plane_at(slot), rows_of(cot_ref[x]))

    def stay(index):
        return taps[:, pl.ds(plane_at(index), WIDTH)]

    five = (0, 1, 2, -1, -2)
    near = (-1, 0, 1)
    own = core_ref[0]
    first = first_ref[0].astype(f32)
    last = last_ref[0].astype(f32)

    def blocks(value, count):
        return [value[i * TAPS : (i + 1) * TAPS] for i in range(count)]

    def padded(value):
        return jnp.concatenate([value, jnp.zeros((value.shape[0], LANES - TAPS), f32)], 1)

    low = stay(0)
    gap = jnp.zeros((LANES - TAPS, WIDTH), bf16)
    top = dot_nt(shifted(taps, 5, five), jnp.concatenate([stay(4), gap, stay(3), gap], 0))
    x1 = blocks(top[:, :LANES], 5)
    x2 = blocks(top[:, LANES:] + dot_nt(shifted(taps, 2, five), jnp.concatenate([low, gap], 0)), 5)
    w_low = dot_nt(shifted(cots, 0, near), low)
    w_high = dot_nt(shifted(cots, 1, near), stay(5))

    def edge(left, right, row):
        return padded(dot_nt(
            taps[:, pl.ds(plane_at(left, row), LANES)], taps[:, pl.ds(plane_at(right, row), LANES)]
        ))

    wide = jnp.zeros((TAPS, LANES - TAPS), f32)
    wsums = (
        wg_ref[0] + jnp.concatenate([w_low, wide], 1),
        wg_ref[1],
        wg_ref[2] + jnp.concatenate([w_high, wide], 1),
    )
    at = lax.broadcasted_iota(jnp.int32, (TAPS, LANES), 1)

    def piece(t):
        if t > GRAD:
            return jnp.zeros((C, LANES), f32)
        if t == GRAD:
            return wsums[1][C : 2 * C]
        a, b, c = t // 9, t // 3 % 3, t % 3
        return pltpu.roll(wsums[a][(2 - b) * C : (3 - b) * C], TAPS - c * C, 1)

    def put(slot, value):
        extra = piece(slot)
        high = extra.astype(bf16).astype(f32)
        extra = jnp.concatenate([high, extra - high, jnp.zeros((C, LANES), f32)], 0)
        out_ref[(slot // HALF) ^ own, slot % HALF] = jnp.where(at < TAPS, value, extra).astype(bf16)

    def cut(value):
        return value

    for base, dx, parts, pairs in (
        (A_X1, 1, x1, ((5, 4),)),
        (A_X2, 2, x2, ((5, 3), (2, 0))),
    ):
        whole = cut(in_ref[base]) + parts[0]
        put(SLOT[(dx, "0")], whole)
        for j, (name, row) in enumerate((("f", 0), ("l", ROWS - 1))):
            edge_sum = cut(in_ref[base + 1 + j])
            for left, right in pairs:
                edge_sum = edge_sum + edge(left, right, row)
            put(SLOT[(dx, name)], whole - edge_sum)
        for j, dy in enumerate((1, 2, -1, -2)):
            put(SLOT[(dx, dy)], cut(in_ref[base + 3 + j]) + parts[1 + j])
    for name in ("0", "f", "l"):
        values = [cut(in_ref[A_X0 + i]) for i in range(5)]
        if name == "f":
            values = [v - first * cut(in_ref[A_P0 + i]) for i, v in enumerate(values)]
        if name == "l":
            values = [v - last * cut(in_ref[A_P3 + i]) for i, v in enumerate(values)]
        put(SLOT[(name, "0")], values[0])
        put(SLOT[(name, "f")], values[0] - values[1])
        put(SLOT[(name, "l")], values[0] - values[2])
        put(SLOT[(name, 1)], values[3])
        put(SLOT[(name, 2)], values[4])
    for slot in range(len(CLASSES), BLOCKS):
        put(slot, jnp.zeros((TAPS, LANES), f32))
    keep_ref[...] = out_ref[0]
    send_ref[...] = out_ref[1]


def settle(value):
    at = lax.broadcasted_iota(jnp.int32, (C, LANES), 1)
    first, second = value[:C], value[C : 2 * C]
    both = first + second
    high = both.astype(bf16).astype(f32)
    first = jnp.where(at < TAPS, first, high)
    second = jnp.where(at < TAPS, second, both - high)
    return jnp.concatenate([first, second, value[2 * C :]], 0).astype(bf16)


def settle_all(value):
    row = lax.broadcasted_iota(jnp.int32, value.shape, value.ndim - 2)
    at = lax.broadcasted_iota(jnp.int32, value.shape, value.ndim - 1)
    swapped = jnp.concatenate(
        [value[..., C : 2 * C, :], value[..., :C, :], value[..., 2 * C :, :]], -2
    )
    both = value + swapped
    high = lax.reduce_precision(both, 8, 7)
    piece = jnp.where(row < C, high, both - high)
    return jnp.where((at < TAPS) | (row >= 2 * C), value, piece).astype(bf16)


def add_kernel(keep_ref, arrived_ref, out_ref):
    for i in range(HALF):
        out_ref[i] = settle(keep_ref[i].astype(f32) + arrived_ref[i].astype(f32))


def sum_kernel(parts_ref, out_ref):
    total = parts_ref[0].astype(f32)
    for i in range(1, parts_ref.shape[0]):
        total = total + parts_ref[i].astype(f32)
    total = settle(total)
    for i in range(out_ref.shape[0]):
        out_ref[i] = total


def conv_kernel(
    odd_ref, act_ref, cot_ref, act_one, act_two, cot_one, cot_two, w_ref,
    out_ref, back_ref,
    act_taps, cot_taps, store, halos, flipped_ref,
):
    step = 2

    def fill(which, index):
        planes, dst = ((act_ref, act_taps), (cot_ref, cot_taps))[which]
        zero_rows(dst, lane(index * RPAD))
        if index in (0, PLANES + 1):
            pair = ((act_one, act_two), (cot_one, cot_two))[which]
            side = index // (PLANES + 1)
            rows = turned(halo_planes(odd_ref[0] == 1, *pair)[side], halos.at[which, side])
        else:
            rows = rows_of(planes[index - 1])
        fill_taps(dst, plane_at(index), rows)

    def products(which, x, weight):
        src = (act_taps, cot_taps)[which]
        plane = store.at[which, x]
        for y in range(0, ROWS, step):
            patch = jnp.concatenate(
                [
                    src[:, pl.ds(plane_at(x + 1 + dx, y + dy), step * LANES)]
                    for dx in (-1, 0, 1)
                    for dy in (-1, 0, 1)
                ],
                0,
            )
            value = jnp.dot(weight, patch, preferred_element_type=f32)
            for i in range(step):
                plane[(y + i) * C : (y + i + 1) * C, :] = value[:, lane(i) : lane(i + 1)]

    def put(which, x):
        target = (out_ref, back_ref)[which]
        for channel in range(C):
            target[channel, x] = store[which, x, pl.ds(channel, ROWS, stride=C), :].astype(bf16)

    flip_taps(w_ref, flipped_ref)
    weights = (w_ref[...], flipped_ref[...])
    fills = [(which, index) for which in (0, 1) for index in range(PLANES + 2)]
    for _ in range(3):
        fill(*fills.pop(0))
    before = None
    for which in (0, 1):
        for x in range(PLANES):
            products(which, x, weights[which])
            for _ in range(2 if which == 0 and x < 3 else 1):
                if fills:
                    fill(*fills.pop(0))
            if before:
                put(*before)
            before = (which, x)
    put(*before)


def split(value):
    high = value.astype(bf16)
    return high, (value - high.astype(f32)).astype(bf16)


def class_of(offset):
    return {0: "0", 1: "f", -1: "l"}[offset]


def finish_kernel(core_ref, mine_ref, other_ref, out_ref, factor):
    own = core_ref[0]

    def chosen(slot, rows=slice(None)):
        here = own == slot // HALF
        return jnp.where(here, mine_ref[slot % HALF, rows, :], other_ref[slot % HALF, rows, :])

    at = lax.broadcasted_iota(jnp.int32, (TAPS, LANES), 1)
    offsets = [(a, b) for a in (-1, 0, 1) for b in (-1, 0, 1)]
    tail = jnp.zeros((LANES - TAPS, LANES), f32)
    diag_row = lax.broadcasted_iota(jnp.int32, (LANES, LANES), 0)
    diag_col = lax.broadcasted_iota(jnp.int32, (LANES, LANES), 1)
    cache = {}

    def size(value):
        return jnp.sum(jnp.abs(value), axis=0, keepdims=True)

    def padded(slot, symmetric):
        if slot not in cache:
            value = jnp.where(at < TAPS, chosen(slot).astype(f32), 0.0)
            full = jnp.concatenate([value, tail], 0)
            turned = full if symmetric else full.T
            cache[slot] = (full.astype(bf16), turned.astype(bf16), size(full), size(turned), full)
        return cache[slot]

    sums = [jnp.zeros((1, LANES), f32) for _ in offsets]
    diagonal = jnp.zeros((LANES, LANES), f32)
    for i, (ax, ay) in enumerate(offsets):
        for j, (bx, by) in enumerate(offsets):
            dx, dy = bx - ax, by - ay
            if dx < 0 or (dx == 0 and dy < 0):
                continue
            key = (class_of(ax) if dx == 0 else dx, class_of(ay) if dy == 0 else dy)
            full, turned, size_full, size_turned, wide = padded(SLOT[key], i == j)
            factor[lane(j) : lane(j + 1), lane(i) : lane(i + 1)] = full
            sums[i] = sums[i] + size_full
            if i != j:
                factor[lane(i) : lane(i + 1), lane(j) : lane(j + 1)] = turned
                sums[j] = sums[j] + size_turned
            else:
                diagonal = diagonal + jnp.where(diag_row == diag_col, wide, 0.0)

    def extra(t):
        return chosen(t, slice(0, C)).astype(f32) + chosen(t, slice(C, 2 * C)).astype(f32)

    pieces = []
    for i in range(9):
        rows = jnp.zeros((C, LANES), f32)
        for c in range(3):
            moved = pltpu.roll(extra(3 * i + c), C + c * C, 1)
            rows = jnp.where(at[:C] // C == c, moved, rows)
        pieces.append(rows)
    wgrad = jnp.concatenate(pieces, 1) * (1.0 / CELLS)

    def exact(left, right):
        return jnp.dot(left, right, precision=lax.Precision.HIGHEST, preferred_element_type=f32)

    grad = extra(GRAD)[:, TAPS:LANES]
    row_id = lax.broadcasted_iota(jnp.int32, (C, C), 0)
    col_id = lax.broadcasted_iota(jnp.int32, (C, C), 1)
    eye = jnp.where(row_id == col_id, 1.0, 0.0).astype(f32)
    scaled = grad * (C / jnp.sum(grad * eye)) + DAMPING * eye
    inverse = eye / jnp.max(jnp.sum(jnp.abs(scaled), axis=1))

    scale = ORDER / jnp.sum(diagonal)
    bound = scale * jnp.max(jnp.concatenate(sums, 0)) + DAMPING
    step = scale / bound
    keep = 1.0 - DAMPING / bound
    value = wgrad
    half = None
    for sweep in range(2**ITERS - 1):
        high, low = split(value)
        product = jnp.dot(jnp.concatenate([high, low], 0), factor[...], preferred_element_type=f32)
        if sweep < 2 * ITERS:
            if sweep % 2 == 0:
                half = exact(inverse, scaled)
            else:
                inverse = 2.0 * inverse - exact(half, inverse)
        value = wgrad + keep * value - step * (product[:C] + product[C:])
    right = value * (1.0 / bound)
    applied = exact(inverse, right)
    quadratic = jnp.sum(applied * wgrad)
    result = applied * jnp.sqrt(C * ORDER / quadratic)
    out_ref[...] = jnp.concatenate([result[:, lane(i) : lane(i) + TAPS] for i in range(9)], 1)


SMEM = pl.BlockSpec(memory_space=pltpu.SMEM)
WHOLE = pl.BlockSpec(memory_space=pltpu.VMEM)
IN_HBM = pl.BlockSpec(memory_space=pltpu.HBM)


def call(kernel, shapes, scratch, inputs, scalars=0, flops=0, mib=16, specs=None, out_specs=None):
    return pl.pallas_call(
        kernel,
        out_shape=shapes,
        in_specs=specs or [SMEM] * scalars + [WHOLE] * (len(inputs) - scalars),
        out_specs=out_specs or jax.tree.map(lambda _: WHOLE, shapes),
        scratch_shapes=scratch,
        compiler_params=pltpu.CompilerParams(vmem_limit_bytes=mib * MIB),
        cost_estimate=pl.CostEstimate(flops=flops, bytes_accessed=1 << 20, transcendentals=0),
    )(*inputs)


def edge_kernel(odd_ref, act, one_ref, two_ref, sems):
    plane = odd_ref[0] * (PLANES - 1)
    copies = [
        pltpu.make_async_copy(act.at[:, plane], one_ref, sems.at[0]),
        pltpu.make_async_copy(act.at[:, PLANES - 1 - plane], two_ref, sems.at[1]),
    ]
    for copy in copies:
        copy.start()
    for copy in copies:
        copy.wait()


def edge_planes(odd, act):
    plane = pltpu.VMEM((C, ROWS, LANES), bf16)
    return call(
        edge_kernel,
        (plane, plane),
        [pltpu.SemaphoreType.DMA((2,))],
        (odd, act),
        mib=4,
        specs=[SMEM, IN_HBM],
    )


def conv(odd, act, cot, halos, weight):
    taps = pltpu.VMEM((TAPS, 6 * RPAD * LANES), bf16)
    shape = jax.ShapeDtypeStruct((C, PLANES, ROWS, LANES), bf16)
    return call(
        conv_kernel,
        (shape, shape),
        [
            taps,
            taps,
            pltpu.VMEM((2, PLANES, C * ROWS, LANES), f32),
            pltpu.VMEM((2, 2, C * ROWS, LANES), f32),
            pltpu.VMEM((C, ORDER), bf16),
        ],
        (odd, act, cot, *halos, weight),
        scalars=1,
        flops=20 * 10**9,
        mib=20,
    )


def body(activations, cotangent, weight):
    space = ("y", "x", "z_lo")
    size = lax.axis_size(space)
    rounds = [
        [pair for i in range(start, size - 1, 2) for pair in ((i, i + 1), (i + 1, i))]
        for start in (0, 1)
    ]
    hold = lax.optimization_barrier

    where = lax.axis_index(space)
    core = lax.axis_index("core").astype(jnp.int32).reshape(1)
    first = (where == 0).astype(jnp.int32).reshape(1)
    last = (where == size - 1).astype(jnp.int32).reshape(1)
    odd = ((where + 1) % 2).astype(jnp.int32).reshape(1)
    activations, cotangent, core, first, last, odd = hold(
        (activations, cotangent, core, first, last, odd)
    )
    act = pltpu.with_memory_space_constraint(activations[0], pltpu.HBM)
    cot = pltpu.with_memory_space_constraint(cotangent[0], pltpu.HBM)
    act_one, act_two = edge_planes(odd, act)
    act_one = lax.ppermute(act_one, space, rounds[0])
    act_two = lax.ppermute(act_two, space, rounds[1])
    turned_shape = pltpu.VMEM((PLANES, ROWS, C, LANES), bf16)
    sums, wsums, turned_act, turned_cot, cot_one, cot_two = call(
        gram_inner,
        (
            pltpu.VMEM((A_BLOCKS, TAPS, LANES), f32),
            pltpu.VMEM((3, TAPS, LANES), f32),
            turned_shape,
            turned_shape,
            jax.ShapeDtypeStruct((C, ROWS, LANES), bf16),
            jax.ShapeDtypeStruct((C, ROWS, LANES), bf16),
        ),
        [
            pltpu.VMEM((TAPS, PLANES * RPAD * LANES), bf16),
            pltpu.VMEM((C, PLANES * RPAD * LANES), bf16),
            pltpu.VMEM((2 * PLANES, C * ROWS, LANES), f32),
            pltpu.VMEM((PLANES, C, ROWS, LANES), bf16),
            pltpu.VMEM((PLANES, C, ROWS, LANES), bf16),
            pltpu.SemaphoreType.DMA((2 * PLANES,)),
        ],
        (odd, act, cot),
        specs=[SMEM, IN_HBM, IN_HBM],
        flops=24 * 10**9 // 4,
        mib=MIB_INNER,
    )
    cot_one = lax.ppermute(cot_one, space, rounds[0])
    cot_two = lax.ppermute(cot_two, space, rounds[1])
    blocks_half = jax.ShapeDtypeStruct((HALF, TAPS, LANES), bf16)
    keep, send = call(
        gram_outer,
        (blocks_half, blocks_half),
        [
            pltpu.VMEM((TAPS, 6 * RPAD * LANES), bf16),
            pltpu.VMEM((C, 2 * RPAD * LANES), bf16),
            pltpu.VMEM((2, HALF, TAPS, LANES), bf16),
            pltpu.VMEM((2, C * ROWS, LANES), f32),
        ],
        (core, first, last, odd, sums, wsums, turned_act, act_one, act_two, turned_cot),
        scalars=4,
        flops=10**9,
        mib=MIB_OUTER,
    )

    swap = [(0, 1), (1, 0)]
    arrived = lax.ppermute(send, "core", swap)
    mine = call(add_kernel, blocks_half, [], (keep, arrived), mib=4)
    parts = lax.all_to_all(mine, ("y", "x"), 0, 0, tiled=True)
    depth = lax.axis_size(("z_hi", "z_lo"))
    block = call(sum_kernel, jax.ShapeDtypeStruct((depth, TAPS, LANES), bf16), [], (parts,), mib=4)
    block, act, cot = hold((block, turned_act, turned_cot))
    parts = lax.all_to_all(block, ("z_hi", "z_lo"), 0, 0, tiled=True)
    halos = (act_one, act_two, cot_one, cot_two)
    out, back = conv(odd, act, cot, halos, weight)
    parts, out, back = hold((parts, out, back))
    block = settle_all(jnp.sum(parts.astype(f32), axis=0))
    block = jnp.broadcast_to(block, (HALF, TAPS, LANES))
    whole = lax.all_to_all(block, ("y", "x"), 0, 0, tiled=True)
    other = lax.ppermute(whole, "core", swap)
    precond = call(
        finish_kernel,
        jax.ShapeDtypeStruct((C, ORDER), f32),
        [pltpu.VMEM((WIDE, WIDE), bf16)],
        (core, whole, other),
        scalars=1,
        flops=10**9,
    )
    return out[None], back[None], precond


def solution(mesh):
    fine = Mesh(mesh.devices.reshape(2, 2, 4, 4, 4), ("z_hi", "core", "y", "x", "z_lo"))
    spec = P(("z_hi", "core"), None, ("y", "x", "z_lo"), None, None)
    return jax.shard_map(
        body,
        mesh=fine,
        in_specs=(spec, spec, P()),
        out_specs=(spec, spec, P()),
        check_vma=False,
    )
```
